256 devices in a mesh: dp: 16 (over y_lo, x, core), cls: 16 (over y_hi, z).
Axes of the slice: x: 4, y: 4 (y_hi: 2, y_lo: 2; y = y_hi * 2 + y_lo), z: 8, core: 2. Of those that a mesh axis runs over, the one named last changes fastest.
Arguments:
- embeddings: bfloat16 [1024, 256], P('dp'), may hold values from -0.75 to 0.75
- labels: int32 [1024], P('dp'), may hold values from 0 to 524287
- centres: bfloat16 [3, 524288, 256], P(None, ('dp', 'cls')), may hold values from -6 to 6
Outputs:
- loss: float32 [], replicated
- grad_embeddings: bfloat16 [1024, 256], P('dp')
- grad_centres: bfloat16 [3, 524288, 256], P(None, ('dp', 'cls'))
The draws below stay inside these ranges and needn't reach their ends.
All inputs are finite; a program needn't handle non-finite values.
Results may differ from the reference program's by a relative error of at most 0.0067.
Values may be sent and summed in bfloat16 or wider, within the bound.
No kernel may reach another device: no remote copies, remote signals or barrier semaphores. Data moves between devices by JAX's collectives and lax.ppermute only.
A program may use at most 64 MiB of HBM per device.

```python
import jax
import jax.numpy as jnp
from jax import lax

E = 256
SUB = 3
BATCH = 1024
CLASSES = 524288


def plant(values, rng, smallest, largest):
    dims = values.shape
    spot = [jax.random.randint(jax.random.fold_in(rng, axis), (), 0, dims[axis]) for axis in range(len(dims))]
    values = values.at[tuple(spot)].set(smallest)
    longest = dims.index(max(dims))
    spot[longest] = (spot[longest] + 1) % dims[longest]
    return values.at[tuple(spot)].set(largest)


def levels(own_key, extent, split, smallest, largest):
    level = 1.0
    for axis_at, blocks in split:
        draws = jax.random.uniform(jax.random.fold_in(jax.random.fold_in(own_key, 6), axis_at), (blocks,), jnp.float32, smallest / len(split), largest / len(split))
        level = level * jnp.repeat(jnp.exp(draws), extent[axis_at] // blocks).reshape((-1,) + (1,) * (len(extent) - 1 - axis_at))
    return level


def scatter_about(own_key, extent, deviation, limit, pieces=(), held_as=jnp.bfloat16):
    values = jax.random.normal(own_key, extent, jnp.float32) * deviation
    if len(pieces) > 0:
        values = levels(own_key, extent, pieces, -0.22, 0.18) * values
    return jnp.clip(values, min=-limit, max=limit).astype(held_as)


def setup_inputs(seed: int = 0) -> dict:
    keys = jax.random.split(jax.random.key(seed), 4)
    return {
        "embeddings": scatter_about(keys[0], (BATCH, E), 0.125, 0.75, ((0, 16),)),
        "labels": plant(jax.random.randint(keys[1], (BATCH,), 0, CLASSES), jax.random.fold_in(keys[1], 1), 0, CLASSES - 1).astype(jnp.int32),
        "centres": scatter_about(keys[2], (SUB, CLASSES, E), 1.0, 6.0, ((1, 256),)),
    }


norm_eps = 1e-06
logit_scale = 30.0
margin_value = 0.2
pool_temp = 0.1

def normalize(values):
    floats = values.astype(jnp.float32)
    width = floats.shape[-1]
    norm_rows = jnp.sqrt(width * (lax.optimization_barrier(jnp.mean(floats * floats, axis=-1, keepdims=True)) + norm_eps))
    return (floats / norm_rows, norm_rows)

def block_terms(unit_rows, unit_cent, labels, first, block):
    cent_block = lax.dynamic_slice_in_dim(unit_cent, first, block, 1)
    cosines = jnp.einsum('be,kce->kbc', unit_rows.astype(jnp.float32), cent_block.astype(jnp.float32))
    weights = jnp.exp(cosines / pool_temp)
    weights = weights / lax.optimization_barrier(jnp.sum(weights, axis=0, keepdims=True))
    pooled = lax.optimization_barrier(jnp.sum(weights * cosines, axis=0))
    columns = first + jnp.arange(block, dtype=jnp.int32)
    onehot = (labels[:, None] == columns[None, :]).astype(jnp.float32)
    logits = logit_scale * (pooled - margin_value * onehot)
    return (cent_block, cosines, weights, pooled, onehot, logits)

def reference(embeddings, labels, centres):
    unit_f, norm_rows = normalize(embeddings)
    unit_rows = unit_f.astype(jnp.bfloat16)
    unit_c_f, norm_c = normalize(centres)
    unit_cent = unit_c_f.astype(jnp.bfloat16)
    total = centres.shape[1]
    block = min(4096, total)
    count = total // block
    rows = embeddings.shape[0]

    def forward(step, carry):
        sums, target = carry
        first = (step * block).astype(jnp.int32)
        terms = block_terms(unit_rows, unit_cent, labels, first, block)
        logits, onehot = (terms[5], terms[4])
        return (sums + lax.optimization_barrier(jnp.sum(jnp.exp(logits), axis=1)), target + lax.optimization_barrier(jnp.sum(logits * onehot, axis=1)))
    zeros = jnp.zeros((rows,), jnp.float32)
    total_exp, target = lax.fori_loop(0, count, forward, (zeros, zeros))
    loss = jnp.mean(jnp.log(total_exp) - target)

    def backward(step, carry):
        grad_unit, grads = carry
        first = (step * block).astype(jnp.int32)
        cent_block, cosines, weights, pooled, onehot, logits = block_terms(unit_rows, unit_cent, labels, first, block)
        dpool = logit_scale * (jnp.exp(logits) / total_exp[:, None] - onehot)
        gcos = (dpool[None] * weights * (1.0 + (cosines - pooled[None]) / pool_temp)).astype(jnp.bfloat16)
        grad_unit = grad_unit + jnp.einsum('kbc,kce->be', gcos.astype(jnp.float32), cent_block.astype(jnp.float32))
        grad_cent = jnp.einsum('kbc,be->kce', gcos.astype(jnp.float32), unit_rows.astype(jnp.float32))
        unit_part = lax.dynamic_slice_in_dim(unit_c_f, first, block, 1)
        norm_part = lax.dynamic_slice_in_dim(norm_c, first, block, 1)
        result = (grad_cent - unit_part * lax.optimization_barrier(jnp.sum(unit_part * grad_cent, axis=-1, keepdims=True))) / norm_part
        grads = lax.dynamic_update_slice_in_dim(grads, result.astype(jnp.bfloat16), first, 1)
        return (grad_unit, grads)
    start = (jnp.zeros(embeddings.shape, jnp.float32), jnp.zeros(centres.shape, jnp.bfloat16))
    grad_unit, grad_centres = lax.fori_loop(0, count, backward, start)
    grad_embeddings = (grad_unit - unit_f * lax.optimization_barrier(jnp.sum(unit_f * grad_unit, axis=-1, keepdims=True))) / norm_rows
    return (loss, grad_embeddings.astype(jnp.bfloat16), grad_centres)
```

```python
import functools
import math

import jax
import jax.numpy as jnp
import numpy as np
from jax import lax
from jax.experimental import pallas as pl
from jax.experimental.pallas import tpu as pltpu
from jax.sharding import Mesh
from jax.sharding import PartitionSpec as P

norm_eps = 1e-06
logit_scale = 30.0
margin_value = 0.2
pool_temp = 0.1

LN2 = math.log(2.0)
A = 1.0 / (pool_temp * LN2)
L = logit_scale * pool_temp
MARGIN2 = logit_scale * margin_value / LN2
INV_LN2 = 1.0 / LN2
OUT_SCALE = logit_scale * LN2

SUB = 3
E = 256
TC = 256
BB = 256
RC = 16
EXTRA = 32

f32 = jnp.float32
bf16 = jnp.bfloat16


def split3(x):
    hi = x.astype(bf16)
    rest = x - hi.astype(f32)
    mid = rest.astype(bf16)
    lo = (rest - mid.astype(f32)).astype(bf16)
    return hi, mid, lo


def inv_norm(floats):
    mean = jnp.sum(floats * floats, axis=-1, keepdims=True) * (1.0 / E)
    return lax.rsqrt(E * (mean + norm_eps))


def send_kernel(slot_ref, emb_ref, lab_ref, out_ref):
    rows = emb_ref[...].astype(f32)
    unit = rows * inv_norm(rows)
    n = rows.shape[0]
    out_ref[pl.ds(0, n), :] = unit.astype(bf16)
    labels = lab_ref[...]
    lane = lax.broadcasted_iota(jnp.int32, (1, E), 1)
    wide = jnp.concatenate([labels] * (E // n), axis=1)
    mine = (lane >= slot_ref[0]) & (lane < slot_ref[0] + n)
    wide = jnp.where(mine, wide, 0)
    row = lax.broadcasted_iota(jnp.int32, (16, E), 0)
    digit = jnp.where(row == 0, wide & 127, jnp.where(row == 1, (wide >> 7) & 127, wide >> 14))
    out_ref[pl.ds(n, 16), :] = jnp.where(row < 3, digit, 0).astype(f32).astype(bf16)


def gather_kernel(rows_own, got_ref, ut_ref, lab_ref):
    parts = got_ref.shape[0]
    per = E // rows_own
    for q in range(parts // per):
        digits = jnp.zeros((16, E), f32)
        for j in range(per):
            digits += got_ref[q * per + j, pl.ds(rows_own, 16), :].astype(f32)
        lab = digits[0:1] + 128.0 * digits[1:2] + 16384.0 * digits[2:3]
        lab_ref[:, pl.ds(q * E, E)] = lab.astype(jnp.int32)
        block = jnp.concatenate(
            [got_ref[q * per + j, pl.ds(0, rows_own), :].astype(f32) for j in range(per)], axis=0
        )
        ut_ref[:, pl.ds(q * E, E)] = block.T.astype(bf16)


def elementwise(c0, c1, c2):
    d1 = (c1 - c0) * A
    d2 = (c2 - c0) * A
    e1 = jnp.exp2(d1)
    e2 = jnp.exp2(d2)
    r = 1.0 / (1.0 + e1 + e2)
    z = (e1 * d1 + e2 * d2) * r
    power = c0 * (L * A) + z * L
    shift = INV_LN2 - z
    return e1, e2, d1, d2, r, power, shift


def forward_kernel(
    first_ref, cent_ref, ut_ref, lab_ref, pt_ref, out_ref, cb, xs, sums, target, g1, g2
):
    step = pl.program_id(0)
    steps = pl.num_programs(0)
    batch = ut_ref.shape[1]

    @pl.when(step == 0)
    def _():
        sums[...] = jnp.zeros_like(sums)
        target[...] = jnp.zeros_like(target)
        g1[...] = jnp.zeros_like(g1)
        g2[...] = jnp.zeros_like(g2)

    for k in range(SUB):
        rows = cent_ref[k].astype(f32)
        cb[pl.ds(k * TC, TC), :] = (rows * inv_norm(rows)).astype(bf16)

    first = first_ref[0] + step * TC
    labels = lab_ref[...] - first
    some = jnp.max(jnp.where((labels >= 0) & (labels < TC), 1, 0)) > 0

    def block(b):
        cols = pl.ds(b * BB, BB)
        xs[b % 2] = jnp.dot(cb[...], ut_ref[:, cols], preferred_element_type=f32)

    def terms(b, labelled):
        cols = pl.ds(b * BB, BB)
        total = jnp.zeros((8, BB), f32)
        tgt = jnp.zeros((8, BB), f32)
        for c in range(TC // RC):
            x = [xs[b % 2, pl.ds(k * TC + c * RC, RC), :] for k in range(SUB)]
            e1, e2, d1, d2, r, power, shift = elementwise(*x)
            if labelled:
                row = lax.broadcasted_iota(jnp.int32, (RC, BB), 0) + c * RC
                hit = row == labels[:, b * BB : (b + 1) * BB]
                power = jnp.where(hit, power - MARGIN2, power)
                t = jnp.where(hit, power, 0.0)
                tgt += t[0:8] + t[8:16]
            ex = jnp.exp2(power)
            total += ex[0:8] + ex[8:16]
            g = ex * r
            p = (g * shift, (g * e1) * (d1 + shift), (g * e2) * (d2 + shift))
            for k in range(SUB):
                pt_ref[k, pl.ds(c * RC, RC), cols] = p[k].astype(bf16)
        sums[:, cols] += total
        if labelled:
            target[:, cols] += tgt

    @pl.when(jnp.logical_not(some))
    def _():
        for b in range(batch // BB):
            block(b)
            terms(b, False)
        for b in range(batch // BB):
            cols = pl.ds(b * BB, BB)
            p = jnp.concatenate([pt_ref[k, :, cols] for k in range(SUB)], axis=0)
            g1[:, cols] += lax.dot_general(
                cb[...], p, (((0,), (0,)), ((), ())), preferred_element_type=f32
            )

    @pl.when(some)
    def _():
        for b in range(batch // BB):
            block(b)
            terms(b, True)
        for b in range(batch // BB):
            cols = pl.ds(b * BB, BB)
            row = lax.broadcasted_iota(jnp.int32, (TC, BB), 0)
            hit = row == labels[:, b * BB : (b + 1) * BB]
            p = [pt_ref[k, :, cols].astype(f32) for k in range(SUB)]
            own = jnp.concatenate([jnp.where(hit, v, 0.0) for v in p], axis=0).astype(bf16)
            rest = jnp.concatenate([jnp.where(hit, 0.0, v) for v in p], axis=0).astype(bf16)
            dims = (((0,), (0,)), ((), ()))
            g1[:, cols] += lax.dot_general(cb[...], rest, dims, preferred_element_type=f32)
            g2[:, cols] += lax.dot_general(cb[...], own, dims, preferred_element_type=f32)

    @pl.when(step == steps - 1)
    def _():
        parts, height = out_ref.shape[0], out_ref.shape[1]
        n = batch // parts
        per = E // n
        tot = jnp.sum(sums[...], axis=0, keepdims=True)
        tgt = jnp.sum(target[...], axis=0, keepdims=True)
        scale = jnp.exp2(-tgt)
        blocks = batch // E
        for q in range(blocks):
            cols = slice(q * E, (q + 1) * E)
            a = g1[:, cols].T.astype(bf16)
            o = (g2[:, cols] * scale[:, cols]).T.astype(bf16)
            for j in range(per):
                out_ref[q * per + j, pl.ds(0, n), :] = a[j * n : (j + 1) * n]
                out_ref[q * per + j, pl.ds(n, n), :] = o[j * n : (j + 1) * n]
        rows = [tot[:, q * E : (q + 1) * E] for q in range(blocks)]
        rows += [tgt[:, q * E : (q + 1) * E] for q in range(blocks)]
        values = jnp.concatenate(rows, axis=0)
        out_extra(out_ref, 2 * n, values)


def out_extra(out_ref, at, values):
    hi, mid, lo = split3(values)
    pad = jnp.zeros((EXTRA - 3 * values.shape[0], E), f32)
    extra = jnp.concatenate(
        [hi.astype(f32), mid.astype(f32), lo.astype(f32), pad], axis=0
    ).astype(bf16)
    if len(out_ref.shape) == 3:
        for j in range(out_ref.shape[0]):
            out_ref[j, pl.ds(at, EXTRA), :] = extra
    else:
        out_ref[pl.ds(at, EXTRA), :] = extra


def summed(got_ref):
    acc = got_ref[0].astype(f32)
    for j in range(1, got_ref.shape[0]):
        acc += got_ref[j].astype(f32)
    return acc


def middle_kernel(n, blocks, got_ref, out_ref):
    acc = summed(got_ref)
    out_ref[pl.ds(0, 2 * n), :] = acc[0 : 2 * n].astype(bf16)
    extra = acc[2 * n :]
    m = 2 * blocks
    values = extra[0:m] + extra[m : 2 * m] + extra[2 * m : 3 * m]
    out_extra(out_ref, 2 * n, values)


def backward_kernel(
    first_ref, got_ref, emb_ref, ut_ref, lab_ref, cent_ref, pt_ref,
    loss_ref, ge_ref, gc_ref, ust, fac,
):
    step = pl.program_id(0)
    batch = ut_ref.shape[1]
    n = emb_ref.shape[0]
    blocks = batch // E

    @pl.when(step == 0)
    def _():
        acc = summed(got_ref)
        extra = acc[2 * n :]
        m = 2 * blocks
        values = extra[0:m] + extra[m : 2 * m] + extra[2 * m : 3 * m]
        tot = jnp.concatenate([values[q : q + 1] for q in range(blocks)], axis=1)
        tgt = jnp.concatenate([values[blocks + q : blocks + q + 1] for q in range(blocks)], axis=1)
        terms = jnp.log(tot) - tgt * LN2
        loss_ref[...] = jnp.sum(terms, axis=1, keepdims=True) * (1.0 / batch)
        inv = OUT_SCALE / tot
        ust[...] = (ut_ref[...].astype(f32) * inv).astype(bf16)
        fac[...] = 1.0 - tot * jnp.exp2(-tgt)
        rows = emb_ref[...].astype(f32)
        r = inv_norm(rows)
        unit = rows * r
        lane = lax.broadcasted_iota(jnp.int32, (n, batch), 1)
        row = lax.broadcasted_iota(jnp.int32, (n, batch), 0)
        mine = lane == row + first_ref[1]
        inv_col = jnp.sum(jnp.where(mine, inv, 0.0), axis=1, keepdims=True)
        own_col = jnp.sum(
            jnp.where(mine, jnp.exp2(tgt) * inv - OUT_SCALE, 0.0), axis=1, keepdims=True
        )
        g = acc[0:n] * inv_col + acc[n : 2 * n] * own_col
        g = (g - unit * jnp.sum(unit * g, axis=1, keepdims=True)) * r
        ge_ref[...] = g.astype(bf16)

    first = first_ref[0] + step * TC
    labels = lab_ref[...] - first
    some = jnp.max(jnp.where((labels >= 0) & (labels < TC), 1, 0)) > 0

    def finish(k, p):
        dims = (((1,), (1,)), ((), ()))
        g = lax.dot_general(p, ust[...], dims, preferred_element_type=f32)
        rows = cent_ref[k].astype(f32)
        r = inv_norm(rows)
        unit = rows * r
        g = (g - unit * jnp.sum(unit * g, axis=1, keepdims=True)) * r
        gc_ref[k] = g.astype(bf16)

    @pl.when(jnp.logical_not(some))
    def _():
        for k in range(SUB):
            finish(k, pt_ref[k])

    @pl.when(some)
    def _():
        hit = lax.broadcasted_iota(jnp.int32, (TC, batch), 0) == labels
        factor = jnp.where(hit, fac[...], 1.0)
        for k in range(SUB):
            finish(k, (pt_ref[k].astype(f32) * factor).astype(bf16))


def per_device(embeddings, labels, centres):
    n = embeddings.shape[0]
    parts = lax.axis_size("dp")
    others = lax.axis_size("cls")
    batch = n * parts
    blocks = batch // E
    local = centres.shape[1]
    steps = local // TC
    dp = lax.axis_index("dp")
    first = (dp * others + lax.axis_index("cls")) * local
    smem = pl.BlockSpec(memory_space=pltpu.SMEM)
    vmem = pl.BlockSpec(memory_space=pltpu.VMEM)
    whole = lambda shape: pl.BlockSpec(shape, lambda i: (0,) * len(shape))
    params = pltpu.CompilerParams(vmem_limit_bytes=48 * 1024 * 1024)

    slot = ((dp % (E // n)) * n).astype(jnp.int32).reshape(1)
    sent = pl.pallas_call(
        send_kernel,
        out_shape=jax.ShapeDtypeStruct((n + 16, E), bf16),
        in_specs=[smem, vmem, vmem],
        out_specs=vmem,
    )(slot, embeddings, labels.reshape(1, n))
    got = lax.all_to_all(jnp.broadcast_to(sent[None], (parts, n + 16, E)), "dp", 0, 0)
    ut, all_labels = pl.pallas_call(
        functools.partial(gather_kernel, n),
        out_shape=(
            jax.ShapeDtypeStruct((E, batch), bf16),
            jax.ShapeDtypeStruct((1, batch), jnp.int32),
        ),
        in_specs=[vmem],
        out_specs=(vmem, vmem),
        compiler_params=params,
    )(got)

    height = 2 * n + EXTRA
    where = jnp.stack([first, dp * n]).astype(jnp.int32)
    pt, payload = pl.pallas_call(
        forward_kernel,
        grid=(steps,),
        out_shape=(
            jax.ShapeDtypeStruct((SUB, local, batch), bf16),
            jax.ShapeDtypeStruct((parts, height, E), bf16),
        ),
        in_specs=[
            smem,
            pl.BlockSpec((SUB, TC, E), lambda i: (0, i, 0)),
            whole((E, batch)),
            whole((1, batch)),
        ],
        out_specs=(
            pl.BlockSpec((SUB, TC, batch), lambda i: (0, i, 0)),
            whole((parts, height, E)),
        ),
        scratch_shapes=[
            pltpu.VMEM((SUB * TC, E), bf16),
            pltpu.VMEM((2, SUB * TC, BB), f32),
            pltpu.VMEM((8, batch), f32),
            pltpu.VMEM((8, batch), f32),
            pltpu.VMEM((E, batch), f32),
            pltpu.VMEM((E, batch), f32),
        ],
        compiler_params=params,
    )(where, centres, ut, all_labels)

    got1 = lax.all_to_all(payload, "dp", 0, 0)
    second = pl.pallas_call(
        functools.partial(middle_kernel, n, blocks),
        out_shape=jax.ShapeDtypeStruct((height, E), bf16),
        in_specs=[vmem],
        out_specs=vmem,
        compiler_params=params,
    )(got1)
    got2 = lax.all_to_all(jnp.broadcast_to(second[None], (others, height, E)), "cls", 0, 0)

    loss, grad_embeddings, grad_centres = pl.pallas_call(
        backward_kernel,
        grid=(steps,),
        out_shape=(
            jax.ShapeDtypeStruct((1, 1), f32),
            jax.ShapeDtypeStruct((n, E), bf16),
            jax.ShapeDtypeStruct((SUB, local, E), bf16),
        ),
        in_specs=[
            smem,
            whole((others, height, E)),
            whole((n, E)),
            whole((E, batch)),
            whole((1, batch)),
            pl.BlockSpec((SUB, TC, E), lambda i: (0, i, 0)),
            pl.BlockSpec((SUB, TC, batch), lambda i: (0, i, 0)),
        ],
        out_specs=(
            whole((1, 1)),
            whole((n, E)),
            pl.BlockSpec((SUB, TC, E), lambda i: (0, i, 0)),
        ),
        scratch_shapes=[pltpu.VMEM((E, batch), bf16), pltpu.VMEM((1, batch), f32)],
        compiler_params=params,
    )(where, got2, embeddings, ut, all_labels, centres, pt)
    return (loss.reshape(()), grad_embeddings, grad_centres)


def solution(mesh):
    return jax.shard_map(
        per_device,
        mesh=mesh,
        in_specs=(P("dp", None), P("dp"), P(None, ("dp", "cls"), None)),
        out_specs=(P(), P("dp", None), P(None, ("dp", "cls"), None)),
        check_vma=False,
    )
```

```python
import functools
import math

import jax
import jax.numpy as jnp
from jax import lax
from jax.experimental import pallas as pl
from jax.experimental.pallas import tpu as pltpu
from jax.sharding import PartitionSpec as P

norm_eps = 1e-06
logit_scale = 30.0
margin_value = 0.2
pool_temp = 0.1

LN2 = math.log(2.0)
A = 1.0 / (pool_temp * LN2)
L = logit_scale * pool_temp
MARGIN2 = logit_scale * margin_value / LN2
INV_LN2 = 1.0 / LN2
OUT_SCALE = logit_scale * LN2

SUB = 3
E = 256
TC = 256
BB = 256
RC = 16
EXTRA = 16

f32 = jnp.float32
bf16 = jnp.bfloat16


def split3(x):
    hi = x.astype(bf16)
    rest = x - hi.astype(f32)
    mid = rest.astype(bf16)
    lo = (rest - mid.astype(f32)).astype(bf16)
    return hi, mid, lo


def inv_norm(floats):
    mean = jnp.sum(floats * floats, axis=-1, keepdims=True) * (1.0 / E)
    return lax.rsqrt(E * (mean + norm_eps))


def send_kernel(slot_ref, emb_ref, lab_ref, out_ref):
    rows = emb_ref[...].astype(f32)
    unit = (rows * inv_norm(rows)).astype(bf16)
    n = rows.shape[0]
    labels = lab_ref[...]
    lane = lax.broadcasted_iota(jnp.int32, (1, E), 1)
    wide = jnp.concatenate([labels] * (E // n), axis=1)
    mine = (lane >= slot_ref[0]) & (lane < slot_ref[0] + n)
    wide = jnp.where(mine, wide, 0)
    row = lax.broadcasted_iota(jnp.int32, (16, E), 0)
    digit = jnp.where(row == 0, wide & 127, jnp.where(row == 1, (wide >> 7) & 127, wide >> 14))
    digit = jnp.where(row < 3, digit, 0).astype(f32).astype(bf16)
    for j in range(out_ref.shape[0]):
        out_ref[j, pl.ds(0, n), :] = unit
        out_ref[j, pl.ds(n, 16), :] = digit


def centre_kernel(cent_ref, cb_ref, cbt_ref):
    for k in range(SUB):
        rows = cent_ref[k].astype(f32)
        unit = rows * inv_norm(rows)
        cb_ref[0, pl.ds(k * TC, TC), :] = unit.astype(bf16)
        cbt_ref[0, :, pl.ds(k * TC, TC)] = unit.T.astype(bf16)


def gather_kernel(rows_own, got_ref, ut_ref, lab_ref):
    parts = got_ref.shape[0]
    per = E // rows_own
    for q in range(parts // per):
        digits = jnp.zeros((16, E), f32)
        for j in range(per):
            digits += got_ref[q * per + j, pl.ds(rows_own, 16), :].astype(f32)
        lab = digits[0:1] + 128.0 * digits[1:2] + 16384.0 * digits[2:3]
        lab_ref[:, pl.ds(q * E, E)] = lab.astype(jnp.int32)
        block = jnp.concatenate(
            [got_ref[q * per + j, pl.ds(0, rows_own), :].astype(f32) for j in range(per)], axis=0
        )
        ut_ref[:, pl.ds(q * E, E)] = block.T.astype(bf16)


def elementwise(c0, c1, c2):
    d1 = (c1 - c0) * A
    d2 = (c2 - c0) * A
    e1 = jnp.exp2(d1)
    e2 = jnp.exp2(d2)
    r = 1.0 / (1.0 + e1 + e2)
    z = (e1 * d1 + e2 * d2) * r
    power = c0 * (L * A) + z * L
    shift = INV_LN2 - z
    return e1, e2, d1, d2, r, power, shift


def forward_kernel(
    first_ref, cb_ref, cbt_ref, ut_ref, lab_ref, pt_ref, out_ref, target, xs, sums, g1, g2
):
    step = pl.program_id(0)
    steps = pl.num_programs(0)
    batch = ut_ref.shape[1]

    @pl.when(step == 0)
    def _():
        sums[...] = jnp.zeros_like(sums)
        target[...] = jnp.zeros_like(target)
        g1[...] = jnp.zeros_like(g1)
        g2[...] = jnp.zeros_like(g2)

    first = first_ref[0] + step * TC
    labels = lab_ref[...] - first
    some = jnp.max(jnp.where((labels >= 0) & (labels < TC), 1, 0)) > 0

    def block(b):
        cols = pl.ds(b * BB, BB)
        xs[b % 2] = jnp.dot(cb_ref[0], ut_ref[:, cols], preferred_element_type=f32)

    def terms(b, labelled):
        cols = pl.ds(b * BB, BB)
        total = jnp.zeros((8, BB), f32)
        tgt = jnp.zeros((8, BB), f32)
        for c in range(TC // RC):
            x = [xs[b % 2, pl.ds(k * TC + c * RC, RC), :] for k in range(SUB)]
            e1, e2, d1, d2, r, power, shift = elementwise(*x)
            if labelled:
                row = lax.broadcasted_iota(jnp.int32, (RC, BB), 0) + c * RC
                hit = row == labels[:, b * BB : (b + 1) * BB]
                power = jnp.where(hit, power - MARGIN2, power)
                t = jnp.where(hit, power, 0.0)
                tgt += t[0:8] + t[8:16]
            ex = jnp.exp2(power)
            total += ex[0:8] + ex[8:16]
            g = ex * r
            p = (g * shift, (g * e1) * (d1 + shift), (g * e2) * (d2 + shift))
            for k in range(SUB):
                pt_ref[k, pl.ds(c * RC, RC), cols] = p[k].astype(bf16)
        sums[:, cols] += total
        if labelled:
            target[:, cols] += tgt

    @pl.when(jnp.logical_not(some))
    def _():
        block(0)
        for b in range(batch // BB):
            cols = pl.ds(b * BB, BB)
            if (b + 1) * BB < batch:
                block(b + 1)
            terms(b, False)
            p = jnp.concatenate([pt_ref[k, :, cols] for k in range(SUB)], axis=0)
            g1[:, cols] += jnp.dot(cbt_ref[0], p, preferred_element_type=f32)

    @pl.when(some)
    def _():
        block(0)
        for b in range(batch // BB):
            cols = pl.ds(b * BB, BB)
            if (b + 1) * BB < batch:
                block(b + 1)
            terms(b, True)
            row = lax.broadcasted_iota(jnp.int32, (TC, BB), 0)
            hit = row == labels[:, b * BB : (b + 1) * BB]
            p = [pt_ref[k, :, cols].astype(f32) for k in range(SUB)]
            own = jnp.concatenate([jnp.where(hit, v, 0.0) for v in p], axis=0).astype(bf16)
            rest = jnp.concatenate([jnp.where(hit, 0.0, v) for v in p], axis=0).astype(bf16)
            g1[:, cols] += jnp.dot(cbt_ref[0], rest, preferred_element_type=f32)
            g2[:, cols] += jnp.dot(cbt_ref[0], own, preferred_element_type=f32)

    @pl.when(step == steps - 1)
    def _():
        parts = out_ref.shape[0]
        n = batch // parts
        per = E // n
        blocks = batch // E
        tot = jnp.sum(sums[...], axis=0, keepdims=True)
        tgt = jnp.sum(target[...], axis=0, keepdims=True)
        scale = jnp.exp2(-tgt)
        all_targets = jnp.sum(tgt, axis=1, keepdims=True)
        totals = jnp.concatenate([tot[:, q * E : (q + 1) * E] for q in range(blocks)], axis=0)
        for q in range(blocks):
            cols = slice(q * E, (q + 1) * E)
            a = g1[:, cols].T.astype(bf16)
            o = (g2[:, cols] * scale[:, cols]).T.astype(bf16)
            extra = pack_extra(totals, tgt[:, cols], all_targets).astype(bf16)
            for j in range(per):
                out_ref[q * per + j, pl.ds(0, n), :] = a[j * n : (j + 1) * n]
                out_ref[q * per + j, pl.ds(n, n), :] = o[j * n : (j + 1) * n]
                out_ref[q * per + j, pl.ds(2 * n, EXTRA), :] = extra


def pack_extra(totals, target, all_targets):
    lane = lax.broadcasted_iota(jnp.int32, (1, E), 1)
    hi, mid, lo = split3(all_targets)
    tail = jnp.where(lane == 0, hi.astype(f32), jnp.where(lane == 1, mid.astype(f32), 0.0))
    tail = jnp.where(lane == 2, lo.astype(f32), tail)
    values = [v.astype(f32) for v in split3(totals)] + [v.astype(f32) for v in split3(target)]
    pad = EXTRA - 3 * totals.shape[0] - 4
    return jnp.concatenate(values + [tail] + [jnp.zeros((pad, E), f32)] * (pad > 0), axis=0)


def unpack_extra(extra, blocks):
    totals = extra[0:blocks] + extra[blocks : 2 * blocks] + extra[2 * blocks : 3 * blocks]
    m = 3 * blocks
    target = extra[m : m + 1] + extra[m + 1 : m + 2] + extra[m + 2 : m + 3]
    all_targets = jnp.sum(extra[m + 3 : m + 4], axis=1, keepdims=True)
    return totals, target, all_targets


def summed(got_ref):
    acc = got_ref[0].astype(f32)
    for j in range(1, got_ref.shape[0]):
        acc += got_ref[j].astype(f32)
    return acc


def middle_kernel(n, blocks, got_ref, out_ref):
    acc = summed(got_ref)
    extra = pack_extra(*unpack_extra(acc[2 * n :], blocks))
    others, height = out_ref.shape[0], out_ref.shape[1]
    m = n // others
    pad = jnp.zeros((height - 2 * m - EXTRA, E), f32)
    for j in range(others):
        one = acc[j * m : (j + 1) * m]
        two = acc[n + j * m : n + (j + 1) * m]
        out_ref[j] = jnp.concatenate([one, two, extra, pad], axis=0).astype(bf16)


def rows_kernel(
    m, where_ref, got_ref, emb_ref, ut_ref, own_ref, loss_ref, ust_ref, fac_ref, rows_ref
):
    batch = ut_ref.shape[1]
    blocks = batch // E
    n = emb_ref.shape[0]
    acc = summed(got_ref)
    totals, target, all_targets = unpack_extra(acc[2 * m : 2 * m + EXTRA], blocks)
    tot = jnp.concatenate([totals[q : q + 1] for q in range(blocks)], axis=1)
    logs = jnp.sum(jnp.log(tot), axis=1, keepdims=True) - all_targets * LN2
    loss_ref[...] = logs * (1.0 / batch)
    inv = OUT_SCALE / tot
    ust_ref[...] = (ut_ref[...].astype(f32) * inv).astype(bf16)
    own = jnp.sum(own_ref[...], axis=0, keepdims=True)
    fac_ref[...] = 1.0 - tot * jnp.exp2(-own)
    lane = lax.broadcasted_iota(jnp.int32, (m, batch), 1)
    row = lax.broadcasted_iota(jnp.int32, (m, batch), 0)
    inv_col = jnp.sum(jnp.where(lane == row + where_ref[1], inv, 0.0), axis=1, keepdims=True)
    lane = lax.broadcasted_iota(jnp.int32, (m, E), 1)
    row = lax.broadcasted_iota(jnp.int32, (m, E), 0)
    mine = lane == row + where_ref[2]
    t = jnp.sum(jnp.where(mine, target, 0.0), axis=1, keepdims=True)
    g = acc[0:m] * inv_col + acc[m : 2 * m] * (jnp.exp2(t) * inv_col - OUT_SCALE)
    lane = lax.broadcasted_iota(jnp.int32, (m, n), 1)
    row = lax.broadcasted_iota(jnp.int32, (m, n), 0)
    pick = jnp.where(lane == row + where_ref[3], 1.0, 0.0).astype(bf16)
    rows = jnp.dot(pick, emb_ref[...], preferred_element_type=f32)
    r = inv_norm(rows)
    unit = rows * r
    g = (g - unit * jnp.sum(unit * g, axis=1, keepdims=True)) * r
    g = jnp.concatenate([g, jnp.zeros((16 - m, E), f32)], axis=0).astype(bf16)
    for j in range(rows_ref.shape[0]):
        rows_ref[j] = g


def collect_kernel(m, got_ref, out_ref):
    parts = [got_ref[j].astype(f32)[0:m] for j in range(got_ref.shape[0])]
    out_ref[...] = jnp.concatenate(parts, axis=0).astype(bf16)


def backward_kernel(first_ref, fac_ref, ust_ref, lab_ref, cent_ref, pt_ref, gc_ref):
    step = pl.program_id(0)
    batch = ust_ref.shape[1]
    first = first_ref[0] + step * TC
    labels = lab_ref[...] - first
    some = jnp.max(jnp.where((labels >= 0) & (labels < TC), 1, 0)) > 0

    def finish(k, p):
        dims = (((1,), (1,)), ((), ()))
        g = lax.dot_general(p, ust_ref[...], dims, preferred_element_type=f32)
        rows = cent_ref[k].astype(f32)
        r = inv_norm(rows)
        unit = rows * r
        g = (g - unit * jnp.sum(unit * g, axis=1, keepdims=True)) * r
        gc_ref[k] = g.astype(bf16)

    @pl.when(jnp.logical_not(some))
    def _():
        for k in range(SUB):
            finish(k, pt_ref[k])

    @pl.when(some)
    def _():
        hit = lax.broadcasted_iota(jnp.int32, (TC, batch), 0) == labels
        factor = jnp.where(hit, fac_ref[...], 1.0)
        for k in range(SUB):
            finish(k, (pt_ref[k].astype(f32) * factor).astype(bf16))


def per_device(embeddings, labels, centres):
    n = embeddings.shape[0]
    parts = lax.axis_size("dp")
    others = lax.axis_size("cls")
    batch = n * parts
    blocks = batch // E
    local = centres.shape[1]
    steps = local // TC
    m = n // others
    dp = lax.axis_index("dp")
    cls = lax.axis_index("cls")
    first = (dp * others + cls) * local
    slot = (dp & (E // n - 1)) * n
    where = jnp.stack([first, dp * n + cls * m, slot + cls * m, cls * m]).astype(jnp.int32)
    smem = pl.BlockSpec(memory_space=pltpu.SMEM)
    vmem = pl.BlockSpec(memory_space=pltpu.VMEM)
    whole = lambda shape: pl.BlockSpec(shape, lambda i: (0,) * len(shape))
    params = pltpu.CompilerParams(vmem_limit_bytes=24 * 1024 * 1024)
    shape = jax.ShapeDtypeStruct

    sent = pl.pallas_call(
        send_kernel,
        out_shape=shape((parts, n + 16, E), bf16),
        in_specs=[smem, vmem, vmem],
        out_specs=vmem,
    )(slot.astype(jnp.int32).reshape(1), embeddings, labels.reshape(1, n))
    got = lax.all_to_all(sent, "dp", 0, 0)
    tile = pl.BlockSpec((SUB, TC, E), lambda i: (0, i, 0))
    rows_tile = pl.BlockSpec((1, SUB * TC, E), lambda i: (i, 0, 0))
    cols_tile = pl.BlockSpec((1, E, SUB * TC), lambda i: (i, 0, 0))
    cb, cbt = pl.pallas_call(
        centre_kernel,
        grid=(steps,),
        out_shape=(shape((steps, SUB * TC, E), bf16), shape((steps, E, SUB * TC), bf16)),
        in_specs=[tile],
        out_specs=(rows_tile, cols_tile),
        compiler_params=params,
        cost_estimate=pl.CostEstimate(flops=10**9, bytes_accessed=10**7, transcendentals=0),
    )(centres)
    ut, all_labels = pl.pallas_call(
        functools.partial(gather_kernel, n),
        out_shape=(shape((E, batch), bf16), shape((1, batch), jnp.int32)),
        in_specs=[vmem],
        out_specs=(vmem, vmem),
        compiler_params=params,
    )(got)

    height = 2 * n + EXTRA
    pt, payload, own_target = pl.pallas_call(
        forward_kernel,
        grid=(steps,),
        out_shape=(
            shape((SUB, local, batch), bf16),
            shape((parts, height, E), bf16),
            shape((8, batch), f32),
        ),
        in_specs=[smem, rows_tile, cols_tile, whole((E, batch)), whole((1, batch))],
        out_specs=(
            pl.BlockSpec((SUB, TC, batch), lambda i: (0, i, 0)),
            whole((parts, height, E)),
            whole((8, batch)),
        ),
        scratch_shapes=[
            pltpu.VMEM((2, SUB * TC, BB), f32),
            pltpu.VMEM((8, batch), f32),
            pltpu.VMEM((E, batch), f32),
            pltpu.VMEM((E, batch), f32),
        ],
        compiler_params=params,
    )(where, cb, cbt, ut, all_labels)

    got1 = lax.all_to_all(payload, "dp", 0, 0)
    second = pl.pallas_call(
        functools.partial(middle_kernel, n, blocks),
        out_shape=shape((others, 32, E), bf16),
        in_specs=[vmem],
        out_specs=vmem,
        compiler_params=params,
    )(got1)
    got2 = lax.all_to_all(second, "cls", 0, 0)
    loss, ust, fac, rows = pl.pallas_call(
        functools.partial(rows_kernel, m),
        out_shape=(
            shape((1, 1), f32),
            shape((E, batch), bf16),
            shape((1, batch), f32),
            shape((others, 16, E), bf16),
        ),
        in_specs=[smem, vmem, vmem, vmem, vmem],
        out_specs=(vmem, vmem, vmem, vmem),
        compiler_params=params,
    )(where, got2, embeddings, ut, own_target)
    got3 = lax.all_to_all(rows, "cls", 0, 0)
    grad_centres = pl.pallas_call(
        backward_kernel,
        grid=(steps,),
        out_shape=shape((SUB, local, E), bf16),
        in_specs=[
            smem,
            whole((1, batch)),
            whole((E, batch)),
            whole((1, batch)),
            tile,
            pl.BlockSpec((SUB, TC, batch), lambda i: (0, i, 0)),
        ],
        out_specs=tile,
        compiler_params=params,
        cost_estimate=pl.CostEstimate(flops=4 * 10**9, bytes_accessed=2 * 10**7, transcendentals=0),
    )(where, fac, ust, all_labels, centres, pt)
    grad_embeddings = pl.pallas_call(
        functools.partial(collect_kernel, m),
        out_shape=shape((n, E), bf16),
        in_specs=[vmem],
        out_specs=vmem,
    )(got3)
    return (loss.reshape(()), grad_embeddings, grad_centres)


def solution(mesh):
    return jax.shard_map(
        per_device,
        mesh=mesh,
        in_specs=(P("dp", None), P("dp"), P(None, ("dp", "cls"), None)),
        out_specs=(P(), P("dp", None), P(None, ("dp", "cls"), None)),
        check_vma=False,
    )
```

```python
import functools
import math

import jax
import jax.numpy as jnp
from jax import lax
from jax.experimental import pallas as pl
from jax.experimental.pallas import tpu as pltpu
from jax.sharding import PartitionSpec as P

norm_eps = 1e-06
logit_scale = 30.0
margin_value = 0.2
pool_temp = 0.1

LN2 = math.log(2.0)
A = 1.0 / (pool_temp * LN2)
L = logit_scale * pool_temp
MARGIN2 = logit_scale * margin_value / LN2
INV_LN2 = 1.0 / LN2
OUT_SCALE = logit_scale * LN2

SUB = 3
E = 256
TC = 512
BB = 256
RC = 16
EXTRA = 16
GROUP = 8

f32 = jnp.float32
bf16 = jnp.bfloat16


def split3(x):
    hi = x.astype(bf16)
    rest = x - hi.astype(f32)
    mid = rest.astype(bf16)
    lo = (rest - mid.astype(f32)).astype(bf16)
    return hi, mid, lo


def inv_norm(floats):
    mean = jnp.sum(floats * floats, axis=-1, keepdims=True) * (1.0 / E)
    return lax.rsqrt(E * (mean + norm_eps))


def send_kernel(slot_ref, emb_ref, lab_ref, out_ref):
    rows = emb_ref[...].astype(f32)
    unit = (rows * inv_norm(rows)).astype(bf16)
    n = rows.shape[0]
    labels = lab_ref[...]
    lane = lax.broadcasted_iota(jnp.int32, (1, E), 1)
    wide = jnp.concatenate([labels] * (E // n), axis=1)
    mine = (lane >= slot_ref[0]) & (lane < slot_ref[0] + n)
    wide = jnp.where(mine, wide, 0)
    row = lax.broadcasted_iota(jnp.int32, (16, E), 0)
    digit = jnp.where(row == 0, wide & 127, jnp.where(row == 1, (wide >> 7) & 127, wide >> 14))
    digit = jnp.where(row < 3, digit, 0).astype(f32).astype(bf16)
    for j in range(out_ref.shape[0]):
        out_ref[j, pl.ds(0, n), :] = unit
        out_ref[j, pl.ds(n, 16), :] = digit


def centre_kernel(cent_ref, cb_ref, cbt_ref):
    for k in range(SUB):
        rows = cent_ref[k].astype(f32)
        unit = rows * inv_norm(rows)
        cb_ref[0, pl.ds(k * TC, TC), :] = unit.astype(bf16)
        cbt_ref[0, :, pl.ds(k * TC, TC)] = unit.T.astype(bf16)


def gather_kernel(rows_own, got_ref, ut_ref, lab_ref):
    parts = got_ref.shape[0]
    per = E // rows_own
    for q in range(parts // per):
        digits = jnp.zeros((16, E), f32)
        for j in range(per):
            digits += got_ref[q * per + j, pl.ds(rows_own, 16), :].astype(f32)
        lab = digits[0:1] + 128.0 * digits[1:2] + 16384.0 * digits[2:3]
        lab_ref[:, pl.ds(q * E, E)] = lab.astype(jnp.int32)
        block = jnp.concatenate(
            [got_ref[q * per + j, pl.ds(0, rows_own), :].astype(f32) for j in range(per)], axis=0
        )
        ut_ref[:, pl.ds(q * E, E)] = block.T.astype(bf16)


def elementwise(c0, c1, c2):
    d1 = (c1 - c0) * A
    d2 = (c2 - c0) * A
    e1 = jnp.exp2(d1)
    e2 = jnp.exp2(d2)
    r = 1.0 / (1.0 + e1 + e2)
    z = (e1 * d1 + e2 * d2) * r
    power = c0 * (L * A) + z * L
    shift = INV_LN2 - z
    return e1, e2, d1, d2, r, power, shift


def forward_kernel(
    first_ref, cb_ref, cbt_ref, ut_ref, lab_ref, pt_ref, out_ref, target, xs, sums, g1, g2
):
    step = pl.program_id(0)
    steps = pl.num_programs(0)
    batch = ut_ref.shape[1]

    @pl.when(step == 0)
    def _():
        sums[...] = jnp.zeros_like(sums)
        target[...] = jnp.zeros_like(target)
        g1[...] = jnp.zeros_like(g1)
        g2[...] = jnp.zeros_like(g2)

    first = first_ref[0] + step * TC
    base = pl.multiple_of(step * TC, TC)
    labels = lab_ref[...] - first
    inside = jnp.where((labels >= 0) & (labels < TC), 1, 0)
    some = jnp.max(inside) > 0

    def block(b):
        cols = pl.ds(b * BB, BB)
        xs[b % 2] = jnp.dot(cb_ref[0], ut_ref[:, cols], preferred_element_type=f32)

    def terms(b, labelled):
        cols = pl.ds(b * BB, BB)
        total = jnp.zeros((8, BB), f32)
        tgt = jnp.zeros((8, BB), f32)
        for c in range(TC // RC):
            x = [xs[b % 2, pl.ds(k * TC + c * RC, RC), :] for k in range(SUB)]
            e1, e2, d1, d2, r, power, shift = elementwise(*x)
            if labelled:
                row = lax.broadcasted_iota(jnp.int32, (RC, BB), 0) + c * RC
                hit = row == labels[:, b * BB : (b + 1) * BB]
                power = jnp.where(hit, power - MARGIN2, power)
                t = jnp.where(hit, power, 0.0)
                tgt += t[0:8] + t[8:16]
            ex = jnp.exp2(power)
            total += ex[0:8] + ex[8:16]
            g = ex * r
            p = (g * shift, (g * e1) * (d1 + shift), (g * e2) * (d2 + shift))
            for k in range(SUB):
                pt_ref[k, pl.ds(base + c * RC, RC), cols] = p[k].astype(bf16)
        sums[:, cols] += total
        if labelled:
            target[:, cols] += tgt

    def rows_sum(b):
        cols = pl.ds(b * BB, BB)
        p = jnp.concatenate([pt_ref[k, pl.ds(base, TC), cols] for k in range(SUB)], axis=0)
        g1[:, cols] += jnp.dot(cbt_ref[0], p, preferred_element_type=f32)

    def rows_sum_labelled(b):
        cols = pl.ds(b * BB, BB)
        row = lax.broadcasted_iota(jnp.int32, (TC, BB), 0)
        hit = row == labels[:, b * BB : (b + 1) * BB]
        for k in range(SUB):
            p = pt_ref[k, pl.ds(base, TC), cols].astype(f32)
            own = jnp.where(hit, p, 0.0).astype(bf16)
            rest = jnp.where(hit, 0.0, p).astype(bf16)
            cbt = cbt_ref[0, :, pl.ds(k * TC, TC)]
            g1[:, cols] += jnp.dot(cbt, rest, preferred_element_type=f32)
            g2[:, cols] += jnp.dot(cbt, own, preferred_element_type=f32)

    @pl.when(jnp.logical_not(some))
    def _():
        block(0)
        for b in range(batch // BB):
            if (b + 1) * BB < batch:
                block(b + 1)
            terms(b, False)
            rows_sum(b)

    @pl.when(some)
    def _():
        for b in range(batch // BB):
            block(b)
            here = jnp.max(inside[:, b * BB : (b + 1) * BB]) > 0

            @pl.when(here)
            def _():
                terms(b, True)
                rows_sum_labelled(b)

            @pl.when(jnp.logical_not(here))
            def _():
                terms(b, False)
                rows_sum(b)

    @pl.when(step == steps - 1)
    def _():
        parts = out_ref.shape[0]
        n = batch // parts
        per = E // n
        blocks = batch // E
        tot = jnp.sum(sums[...], axis=0, keepdims=True)
        tgt = jnp.sum(target[...], axis=0, keepdims=True)
        scale = jnp.exp2(-tgt)
        all_targets = jnp.sum(tgt, axis=1, keepdims=True)
        totals = jnp.concatenate([tot[:, q * E : (q + 1) * E] for q in range(blocks)], axis=0)
        for q in range(blocks):
            cols = slice(q * E, (q + 1) * E)
            a = g1[:, cols].T.astype(bf16)
            o = (g2[:, cols] * scale[:, cols]).T.astype(bf16)
            extra = pack_extra(totals, tgt[:, cols], all_targets).astype(bf16)
            for j in range(per):
                out_ref[q * per + j, pl.ds(0, n), :] = a[j * n : (j + 1) * n]
                out_ref[q * per + j, pl.ds(n, n), :] = o[j * n : (j + 1) * n]
                out_ref[q * per + j, pl.ds(2 * n, EXTRA), :] = extra


def pack_extra(totals, target, all_targets):
    lane = lax.broadcasted_iota(jnp.int32, (1, E), 1)
    hi, mid, lo = split3(all_targets)
    tail = jnp.where(lane == 0, hi.astype(f32), jnp.where(lane == 1, mid.astype(f32), 0.0))
    tail = jnp.where(lane == 2, lo.astype(f32), tail)
    values = [v.astype(f32) for v in split3(totals)] + [v.astype(f32) for v in split3(target)]
    pad = EXTRA - 3 * totals.shape[0] - 4
    return jnp.concatenate(values + [tail] + [jnp.zeros((pad, E), f32)] * (pad > 0), axis=0)


def unpack_extra(extra, blocks):
    totals = extra[0:blocks] + extra[blocks : 2 * blocks] + extra[2 * blocks : 3 * blocks]
    m = 3 * blocks
    target = extra[m : m + 1] + extra[m + 1 : m + 2] + extra[m + 2 : m + 3]
    all_targets = jnp.sum(extra[m + 3 : m + 4], axis=1, keepdims=True)
    return totals, target, all_targets


def summed(got_ref):
    acc = got_ref[0].astype(f32)
    for j in range(1, got_ref.shape[0]):
        acc += got_ref[j].astype(f32)
    return acc


def middle_kernel(n, blocks, got_ref, out_ref):
    acc = summed(got_ref)
    extra = pack_extra(*unpack_extra(acc[2 * n :], blocks))
    others, height = out_ref.shape[0], out_ref.shape[1]
    m = n // GROUP
    pad = jnp.zeros((height - 2 * m - EXTRA, E), f32)
    for j in range(others):
        at = (j % GROUP) * m
        one = acc[at : at + m]
        two = acc[n + at : n + at + m]
        out_ref[j] = jnp.concatenate([one, two, extra] + [pad] * (pad.shape[0] > 0), axis=0).astype(bf16)


def rows_kernel(
    m, where_ref, got_ref, emb_ref, ut_ref, own_ref, loss_ref, ust_ref, fac_ref, rows_ref
):
    batch = ut_ref.shape[1]
    blocks = batch // E
    n = emb_ref.shape[0]
    acc = summed(got_ref)
    totals, target, all_targets = unpack_extra(acc[2 * m : 2 * m + EXTRA], blocks)
    tot = jnp.concatenate([totals[q : q + 1] for q in range(blocks)], axis=1)
    logs = jnp.sum(jnp.log(tot), axis=1, keepdims=True) - all_targets * LN2
    loss_ref[...] = logs * (1.0 / batch)
    inv = OUT_SCALE / tot
    ust_ref[...] = (ut_ref[...].astype(f32) * inv).astype(bf16)
    own = jnp.sum(own_ref[...], axis=0, keepdims=True)
    fac_ref[...] = 1.0 - tot * jnp.exp2(-own)
    lane = lax.broadcasted_iota(jnp.int32, (m, batch), 1)
    row = lax.broadcasted_iota(jnp.int32, (m, batch), 0)
    inv_col = jnp.sum(jnp.where(lane == row + where_ref[1], inv, 0.0), axis=1, keepdims=True)
    lane = lax.broadcasted_iota(jnp.int32, (m, E), 1)
    row = lax.broadcasted_iota(jnp.int32, (m, E), 0)
    mine = lane == row + where_ref[2]
    t = jnp.sum(jnp.where(mine, target, 0.0), axis=1, keepdims=True)
    g = acc[0:m] * inv_col + acc[m : 2 * m] * (jnp.exp2(t) * inv_col - OUT_SCALE)
    lane = lax.broadcasted_iota(jnp.int32, (m, n), 1)
    row = lax.broadcasted_iota(jnp.int32, (m, n), 0)
    pick = jnp.where(lane == row + where_ref[3], 1.0, 0.0).astype(bf16)
    rows = jnp.dot(pick, emb_ref[...], preferred_element_type=f32)
    r = inv_norm(rows)
    unit = rows * r
    g = (g - unit * jnp.sum(unit * g, axis=1, keepdims=True)) * r
    for j in range(rows_ref.shape[0]):
        rows_ref[j] = g.astype(bf16)


def backward_kernel(
    first_ref, fac_ref, ust_ref, lab_ref, got_ref, cent_ref, pt_ref, ge_ref, gc_ref
):
    step = pl.program_id(0)
    batch = ust_ref.shape[1]
    first = first_ref[0] + step * TC
    base = pl.multiple_of(step * TC, TC)
    labels = lab_ref[...] - first
    some = jnp.max(jnp.where((labels >= 0) & (labels < TC), 1, 0)) > 0

    @pl.when(step == 0)
    def _():
        parts = [got_ref[j].astype(f32) for j in range(got_ref.shape[0])]
        ge_ref[...] = jnp.concatenate(parts, axis=0).astype(bf16)

    def finish(k, p):
        dims = (((1,), (1,)), ((), ()))
        g = lax.dot_general(p, ust_ref[...], dims, preferred_element_type=f32)
        rows = cent_ref[k].astype(f32)
        r = inv_norm(rows)
        unit = rows * r
        g = (g - unit * jnp.sum(unit * g, axis=1, keepdims=True)) * r
        gc_ref[k] = g.astype(bf16)

    @pl.when(jnp.logical_not(some))
    def _():
        for k in range(SUB):
            finish(k, pt_ref[k, pl.ds(base, TC), :])

    @pl.when(some)
    def _():
        hit = lax.broadcasted_iota(jnp.int32, (TC, batch), 0) == labels
        factor = jnp.where(hit, fac_ref[...], 1.0)
        for k in range(SUB):
            finish(k, (pt_ref[k, pl.ds(base, TC), :].astype(f32) * factor).astype(bf16))


def per_device(embeddings, labels, centres):
    n = embeddings.shape[0]
    parts = lax.axis_size("dp")
    others = lax.axis_size("cls")
    batch = n * parts
    blocks = batch // E
    local = centres.shape[1]
    steps = local // TC
    m = n // GROUP
    dp = lax.axis_index("dp")
    cls = lax.axis_index("cls")
    first = (dp * others + cls) * local
    slot = (dp & (E // n - 1)) * n
    at = (cls & (GROUP - 1)) * m
    where = jnp.stack([first, dp * n + at, slot + at, at]).astype(jnp.int32)
    smem = pl.BlockSpec(memory_space=pltpu.SMEM)
    vmem = pl.BlockSpec(memory_space=pltpu.VMEM)
    whole = lambda shape: pl.BlockSpec(shape, lambda i: (0,) * len(shape))
    params = pltpu.CompilerParams(vmem_limit_bytes=24 * 1024 * 1024)
    shape = jax.ShapeDtypeStruct

    sent = pl.pallas_call(
        send_kernel,
        out_shape=shape((parts, n + 16, E), bf16),
        in_specs=[smem, vmem, vmem],
        out_specs=vmem,
    )(slot.astype(jnp.int32).reshape(1), embeddings, labels.reshape(1, n))
    got = lax.all_to_all(sent, "dp", 0, 0)
    tile = pl.BlockSpec((SUB, TC, E), lambda i: (0, i, 0))
    rows_tile = pl.BlockSpec((1, SUB * TC, E), lambda i: (i, 0, 0))
    cols_tile = pl.BlockSpec((1, E, SUB * TC), lambda i: (i, 0, 0))
    cb, cbt = pl.pallas_call(
        centre_kernel,
        grid=(steps,),
        out_shape=(shape((steps, SUB * TC, E), bf16), shape((steps, E, SUB * TC), bf16)),
        in_specs=[tile],
        out_specs=(rows_tile, cols_tile),
        compiler_params=params,
        cost_estimate=pl.CostEstimate(flops=10**9, bytes_accessed=10**7, transcendentals=0),
    )(centres)
    ut, all_labels = pl.pallas_call(
        functools.partial(gather_kernel, n),
        out_shape=(shape((E, batch), bf16), shape((1, batch), jnp.int32)),
        in_specs=[vmem],
        out_specs=(vmem, vmem),
        compiler_params=params,
    )(got)

    height = 2 * n + EXTRA
    pt, payload, own_target = pl.pallas_call(
        forward_kernel,
        grid=(steps,),
        out_shape=(
            shape((SUB, local, batch), bf16),
            shape((parts, height, E), bf16),
            shape((8, batch), f32),
        ),
        in_specs=[smem, rows_tile, cols_tile, whole((E, batch)), whole((1, batch))],
        out_specs=(
            vmem,
            whole((parts, height, E)),
            whole((8, batch)),
        ),
        scratch_shapes=[
            pltpu.VMEM((2, SUB * TC, BB), f32),
            pltpu.VMEM((8, batch), f32),
            pltpu.VMEM((E, batch), f32),
            pltpu.VMEM((E, batch), f32),
        ],
        compiler_params=params,
    )(where, cb, cbt, ut, all_labels)

    got1 = lax.all_to_all(payload, "dp", 0, 0)
    second = pl.pallas_call(
        functools.partial(middle_kernel, n, blocks),
        out_shape=shape((others, 32, E), bf16),
        in_specs=[vmem],
        out_specs=vmem,
        compiler_params=params,
    )(got1)
    got2 = lax.all_to_all(second, "cls", 0, 0)
    loss, ust, fac, rows = pl.pallas_call(
        functools.partial(rows_kernel, m),
        out_shape=(
            shape((1, 1), f32),
            shape((E, batch), bf16),
            shape((1, batch), f32),
            shape((GROUP, m, E), bf16),
        ),
        in_specs=[smem, vmem, vmem, vmem, vmem],
        out_specs=(vmem, vmem, vmem, vmem),
        compiler_params=params,
    )(where, got2, embeddings, ut, own_target)
    groups = [list(range(g, g + GROUP)) for g in range(0, others, GROUP)]
    got3 = lax.all_to_all(rows, "cls", 0, 0, axis_index_groups=groups)
    grad_embeddings, grad_centres = pl.pallas_call(
        backward_kernel,
        grid=(steps,),
        out_shape=(shape((n, E), bf16), shape((SUB, local, E), bf16)),
        in_specs=[
            smem,
            whole((1, batch)),
            whole((E, batch)),
            whole((1, batch)),
            whole((GROUP, m, E)),
            tile,
            vmem,
        ],
        out_specs=(whole((n, E)), tile),
        compiler_params=params,
    )(where, fac, ust, all_labels, got3, centres, pt)
    return (loss.reshape(()), grad_embeddings, grad_centres)


def solution(mesh):
    return jax.shard_map(
        per_device,
        mesh=mesh,
        in_specs=(P("dp", None), P("dp"), P(None, ("dp", "cls"), None)),
        out_specs=(P(), P("dp", None), P(None, ("dp", "cls"), None)),
        check_vma=False,
    )
```

```python
import functools
import math

import jax
import jax.numpy as jnp
from jax import lax
from jax.experimental import pallas as pl
from jax.experimental.pallas import tpu as pltpu
from jax.sharding import PartitionSpec as P

norm_eps = 1e-06
logit_scale = 30.0
margin_value = 0.2
pool_temp = 0.1

LN2 = math.log(2.0)
A = 1.0 / (pool_temp * LN2)
L = logit_scale * pool_temp
MARGIN2 = logit_scale * margin_value / LN2
INV_LN2 = 1.0 / LN2
OUT_SCALE = logit_scale * LN2

SUB = 3
E = 256
TC = 512
BB = 256
FT = 256
RC = 16
AWAY = -1e4
EXTRA = 16
GROUP = 8

f32 = jnp.float32
bf16 = jnp.bfloat16


def split3(x):
    hi = x.astype(bf16)
    rest = x - hi.astype(f32)
    mid = rest.astype(bf16)
    lo = (rest - mid.astype(f32)).astype(bf16)
    return hi, mid, lo


def inv_norm(floats):
    mean = jnp.sum(floats * floats, axis=-1, keepdims=True) * (1.0 / E)
    return lax.rsqrt(E * (mean + norm_eps))


def send_kernel(slot_ref, emb_ref, lab_ref, out_ref):
    rows = emb_ref[...].astype(f32)
    unit = (rows * inv_norm(rows)).astype(bf16)
    n = rows.shape[0]
    labels = lab_ref[...]
    lane = lax.broadcasted_iota(jnp.int32, (1, E), 1)
    wide = jnp.concatenate([labels] * (E // n), axis=1)
    mine = (lane >= slot_ref[0]) & (lane < slot_ref[0] + n)
    wide = jnp.where(mine, wide, 0)
    row = lax.broadcasted_iota(jnp.int32, (16, E), 0)
    digit = jnp.where(row == 0, wide & 127, jnp.where(row == 1, (wide >> 7) & 127, wide >> 14))
    digit = jnp.where(row < 3, digit, 0).astype(f32).astype(bf16)
    for j in range(out_ref.shape[0]):
        out_ref[j, pl.ds(0, n), :] = unit
        out_ref[j, pl.ds(n, 16), :] = digit


def centre_kernel(cent_ref, cb_ref, cbt_ref):
    for k in range(SUB):
        rows = cent_ref[k].astype(f32)
        unit = rows * inv_norm(rows)
        cb_ref[0, pl.ds(k * TC, TC), :] = unit.astype(bf16)
        cbt_ref[0, :, pl.ds(k * TC, TC)] = unit.T.astype(bf16)


def gather_kernel(rows_own, where_ref, got_ref, ut_ref, lab_ref, flag_ref):
    parts = got_ref.shape[0]
    per = E // rows_own
    for q in range(parts // per):
        digits = jnp.zeros((16, E), f32)
        for j in range(per):
            digits += got_ref[q * per + j, pl.ds(rows_own, 16), :].astype(f32)
        lab = digits[0:1] + 128.0 * digits[1:2] + 16384.0 * digits[2:3]
        lab_ref[:, pl.ds(q * E, E)] = lab.astype(jnp.int32)
        block = jnp.concatenate(
            [got_ref[q * per + j, pl.ds(0, rows_own), :].astype(f32) for j in range(per)], axis=0
        )
        ut_ref[:, pl.ds(q * E, E)] = block.T.astype(bf16)
    tiles, width = flag_ref.shape
    batch = lab_ref.shape[1]
    tile = (lab_ref[...] - where_ref[0]) >> (FT.bit_length() - 1)
    hits = (lax.broadcasted_iota(jnp.int32, (tiles, batch), 0) == tile).astype(f32)
    lane = lax.broadcasted_iota(jnp.int32, (tiles, width), 1)
    flags = jnp.zeros((tiles, width), f32)
    for b in range(batch // BB):
        count = jnp.sum(hits[:, b * BB : (b + 1) * BB], axis=1, keepdims=True)
        flags = jnp.where(lane == b, count, flags)
    flag_ref[...] = flags.astype(jnp.int32)


def elementwise(c0, c1, c2):
    d1 = (c1 - c0) * A
    d2 = (c2 - c0) * A
    e1 = jnp.exp2(d1)
    e2 = jnp.exp2(d2)
    r = 1.0 / (1.0 + e1 + e2)
    z = (e1 * d1 + e2 * d2) * r
    power = c0 * (L * A) + z * L
    shift = INV_LN2 - z
    return e1, e2, d1, d2, r, power, shift


def forward_kernel(
    first_ref, flag_ref, cb_ref, cbt_ref, ut_ref, lab_ref,
    pt_ref, out_ref, target, own_ref, xs, sums, g1, g2,
):
    step = pl.program_id(0)
    steps = pl.num_programs(0)
    batch = ut_ref.shape[1]

    @pl.when(step == 0)
    def _():
        sums[...] = jnp.zeros_like(sums)
        target[...] = jnp.zeros_like(target)
        own_ref[...] = jnp.zeros_like(own_ref)
        g1[...] = jnp.zeros_like(g1)
        g2[...] = jnp.zeros_like(g2)

    first = first_ref[0] + step * TC
    base = pl.multiple_of(step * TC, TC)

    def block(b):
        cols = pl.ds(b * BB, BB)
        xs[b % 2] = jnp.dot(cb_ref[0], ut_ref[:, cols], preferred_element_type=f32)

    def set_labels_apart(b, h):
        cols = pl.ds(b * BB, BB)
        row = lax.broadcasted_iota(jnp.int32, (FT, BB), 0) + h * FT
        hit = row == lab_ref[:, cols] - first
        known = jnp.sum(jnp.where(hit, 1.0, 0.0), axis=0, keepdims=True) > 0
        x = []
        for k in range(SUB):
            rows = pl.ds(k * TC + h * FT, FT)
            v = xs[b % 2, rows, :]
            x.append(jnp.sum(jnp.where(hit, v, 0.0), axis=0, keepdims=True))
            xs[b % 2, rows, :] = jnp.where(hit, AWAY, v)
        e1, e2, d1, d2, r, power, shift = elementwise(*x)
        power = power - MARGIN2
        target[0:1, cols] += jnp.where(known, power, 0.0)
        sums[0:1, cols] += jnp.where(known, jnp.exp2(power), 0.0)
        p = (r * shift, (r * e1) * (d1 + shift), (r * e2) * (d2 + shift))
        for k in range(SUB):
            own_ref[k : k + 1, cols] += jnp.where(known, p[k], 0.0)
            own = jnp.where(hit, p[k], 0.0).astype(bf16)
            cbt = cbt_ref[0, :, pl.ds(k * TC + h * FT, FT)]
            g2[:, cols] += jnp.dot(cbt, own, preferred_element_type=f32)

    def terms(b):
        cols = pl.ds(b * BB, BB)
        total = jnp.zeros((8, BB), f32)
        for c in range(TC // RC):
            x = [xs[b % 2, pl.ds(k * TC + c * RC, RC), :] for k in range(SUB)]
            e1, e2, d1, d2, r, power, shift = elementwise(*x)
            ex = jnp.exp2(power)
            total += ex[0:8] + ex[8:16]
            g = ex * r
            p = (g * shift, (g * e1) * (d1 + shift), (g * e2) * (d2 + shift))
            for k in range(SUB):
                pt_ref[k, pl.ds(base + c * RC, RC), cols] = p[k].astype(bf16)
        sums[:, cols] += total

    def rows_sum(b):
        cols = pl.ds(b * BB, BB)
        p = jnp.concatenate([pt_ref[k, pl.ds(base, TC), cols] for k in range(SUB)], axis=0)
        g1[:, cols] += jnp.dot(cbt_ref[0], p, preferred_element_type=f32)

    block(0)
    for b in range(batch // BB):
        for h in range(TC // FT):
            pl.when(flag_ref[step * (TC // FT) + h, b] > 0)(
                functools.partial(set_labels_apart, b, h)
            )
        if (b + 1) * BB < batch:
            block(b + 1)
        terms(b)
        rows_sum(b)

    @pl.when(step == steps - 1)
    def _():
        parts = out_ref.shape[0]
        n = batch // parts
        per = E // n
        blocks = batch // E
        tot = jnp.sum(sums[...], axis=0, keepdims=True)
        tgt = jnp.sum(target[...], axis=0, keepdims=True)
        all_targets = jnp.sum(tgt, axis=1, keepdims=True)
        totals = jnp.concatenate([tot[:, q * E : (q + 1) * E] for q in range(blocks)], axis=0)
        for q in range(blocks):
            cols = slice(q * E, (q + 1) * E)
            a = g1[:, cols].T.astype(bf16)
            o = g2[:, cols].T.astype(bf16)
            extra = pack_extra(totals, tgt[:, cols], all_targets).astype(bf16)
            for j in range(per):
                out_ref[q * per + j, pl.ds(0, n), :] = a[j * n : (j + 1) * n]
                out_ref[q * per + j, pl.ds(n, n), :] = o[j * n : (j + 1) * n]
                out_ref[q * per + j, pl.ds(2 * n, EXTRA), :] = extra


def pack_extra(totals, target, all_targets):
    lane = lax.broadcasted_iota(jnp.int32, (1, E), 1)
    hi, mid, lo = split3(all_targets)
    tail = jnp.where(lane == 0, hi.astype(f32), jnp.where(lane == 1, mid.astype(f32), 0.0))
    tail = jnp.where(lane == 2, lo.astype(f32), tail)
    values = [v.astype(f32) for v in split3(totals)] + [v.astype(f32) for v in split3(target)]
    pad = EXTRA - 3 * totals.shape[0] - 4
    return jnp.concatenate(values + [tail] + [jnp.zeros((pad, E), f32)] * (pad > 0), axis=0)


def unpack_extra(extra, blocks):
    totals = extra[0:blocks] + extra[blocks : 2 * blocks] + extra[2 * blocks : 3 * blocks]
    m = 3 * blocks
    target = extra[m : m + 1] + extra[m + 1 : m + 2] + extra[m + 2 : m + 3]
    all_targets = jnp.sum(extra[m + 3 : m + 4], axis=1, keepdims=True)
    return totals, target, all_targets


def summed(got_ref):
    acc = got_ref[0].astype(f32)
    for j in range(1, got_ref.shape[0]):
        acc += got_ref[j].astype(f32)
    return acc


def middle_kernel(n, blocks, got_ref, out_ref):
    acc = summed(got_ref)
    extra = pack_extra(*unpack_extra(acc[2 * n :], blocks))
    others, height = out_ref.shape[0], out_ref.shape[1]
    m = n // GROUP
    pad = jnp.zeros((height - 2 * m - EXTRA, E), f32)
    for j in range(others):
        at = (j % GROUP) * m
        one = acc[at : at + m]
        two = acc[n + at : n + at + m]
        out_ref[j] = jnp.concatenate([one, two, extra] + [pad] * (pad.shape[0] > 0), axis=0).astype(bf16)


def rows_kernel(
    m, where_ref, got_ref, emb_ref, ut_ref, target_ref, own_ref,
    loss_ref, ust_ref, fac_ref, rows_ref,
):
    batch = ut_ref.shape[1]
    blocks = batch // E
    n = emb_ref.shape[0]
    acc = summed(got_ref)
    totals, target, all_targets = unpack_extra(acc[2 * m : 2 * m + EXTRA], blocks)
    tot = jnp.concatenate([totals[q : q + 1] for q in range(blocks)], axis=1)
    logs = jnp.sum(jnp.log(tot), axis=1, keepdims=True) - all_targets * LN2
    loss_ref[...] = logs * (1.0 / batch)
    inv = OUT_SCALE / tot
    ust_ref[...] = (ut_ref[...].astype(f32) * inv).astype(bf16)
    own_target = jnp.sum(target_ref[...], axis=0, keepdims=True)
    fac_ref[...] = own_ref[...] * (jnp.exp2(own_target) - tot)
    lane = lax.broadcasted_iota(jnp.int32, (m, batch), 1)
    row = lax.broadcasted_iota(jnp.int32, (m, batch), 0)
    inv_col = jnp.sum(jnp.where(lane == row + where_ref[1], inv, 0.0), axis=1, keepdims=True)
    lane = lax.broadcasted_iota(jnp.int32, (m, E), 1)
    row = lax.broadcasted_iota(jnp.int32, (m, E), 0)
    mine = lane == row + where_ref[2]
    t = jnp.sum(jnp.where(mine, target, 0.0), axis=1, keepdims=True)
    g = acc[0:m] * inv_col + acc[m : 2 * m] * (jnp.exp2(t) * inv_col - OUT_SCALE)
    lane = lax.broadcasted_iota(jnp.int32, (m, n), 1)
    row = lax.broadcasted_iota(jnp.int32, (m, n), 0)
    pick = jnp.where(lane == row + where_ref[3], 1.0, 0.0).astype(bf16)
    rows = jnp.dot(pick, emb_ref[...], preferred_element_type=f32)
    r = inv_norm(rows)
    unit = rows * r
    g = (g - unit * jnp.sum(unit * g, axis=1, keepdims=True)) * r
    for j in range(rows_ref.shape[0]):
        rows_ref[j] = g.astype(bf16)


def backward_kernel(
    first_ref, flag_ref, fac_ref, ust_ref, lab_ref, got_ref, cent_ref, pt_ref, ge_ref, gc_ref, gs
):
    step = pl.program_id(0)
    batch = ust_ref.shape[1]
    first = first_ref[0] + step * TC
    base = pl.multiple_of(step * TC, TC)
    dims = (((1,), (1,)), ((), ()))

    @pl.when(step == 0)
    def _():
        parts = [got_ref[j].astype(f32) for j in range(got_ref.shape[0])]
        ge_ref[...] = jnp.concatenate(parts, axis=0).astype(bf16)

    def product(k):
        return lax.dot_general(
            pt_ref[k, pl.ds(base, TC), :], ust_ref[...], dims, preferred_element_type=f32
        )

    def finish(k, g):
        rows = cent_ref[k].astype(f32)
        r = inv_norm(rows)
        unit = rows * r
        g = (g - unit * jnp.sum(unit * g, axis=1, keepdims=True)) * r
        gc_ref[k] = g.astype(bf16)

    def add_labels(b, h):
        cols = pl.ds(b * BB, BB)
        row = lax.broadcasted_iota(jnp.int32, (FT, BB), 0) + h * FT
        hit = row == lab_ref[:, cols] - first
        for k in range(SUB):
            own = jnp.where(hit, fac_ref[k : k + 1, cols], 0.0).astype(bf16)
            gs[k, pl.ds(h * FT, FT), :] += lax.dot_general(
                own, ust_ref[:, cols], dims, preferred_element_type=f32
            )

    flags = [
        (b, h, flag_ref[step * (TC // FT) + h, b])
        for b in range(batch // BB)
        for h in range(TC // FT)
    ]
    some = sum(f for _, _, f in flags) > 0

    @pl.when(jnp.logical_not(some))
    def _():
        for k in range(SUB):
            finish(k, product(k))

    @pl.when(some)
    def _():
        for k in range(SUB):
            gs[k] = product(k)
        for b, h, flag in flags:
            pl.when(flag > 0)(functools.partial(add_labels, b, h))
        for k in range(SUB):
            finish(k, gs[k])


def per_device(embeddings, labels, centres):
    n = embeddings.shape[0]
    parts = lax.axis_size("dp")
    others = lax.axis_size("cls")
    batch = n * parts
    blocks = batch // E
    local = centres.shape[1]
    steps = local // TC
    m = n // GROUP
    dp = lax.axis_index("dp")
    cls = lax.axis_index("cls")
    first = (dp * others + cls) * local
    slot = (dp & (E // n - 1)) * n
    at = (cls & (GROUP - 1)) * m
    where = jnp.stack([first, dp * n + at, slot + at, at]).astype(jnp.int32)
    smem = pl.BlockSpec(memory_space=pltpu.SMEM)
    vmem = pl.BlockSpec(memory_space=pltpu.VMEM)
    whole = lambda shape: pl.BlockSpec(shape, lambda i: (0,) * len(shape))
    params = pltpu.CompilerParams(vmem_limit_bytes=24 * 1024 * 1024)
    shape = jax.ShapeDtypeStruct

    sent = pl.pallas_call(
        send_kernel,
        out_shape=shape((parts, n + 16, E), bf16),
        in_specs=[smem, vmem, vmem],
        out_specs=vmem,
    )(slot.astype(jnp.int32).reshape(1), embeddings, labels.reshape(1, n))
    got = lax.all_to_all(sent, "dp", 0, 0)
    tile = pl.BlockSpec((SUB, TC, E), lambda i: (0, i, 0))
    rows_tile = pl.BlockSpec((1, SUB * TC, E), lambda i: (i, 0, 0))
    cols_tile = pl.BlockSpec((1, E, SUB * TC), lambda i: (i, 0, 0))
    cb, cbt = pl.pallas_call(
        centre_kernel,
        grid=(steps,),
        out_shape=(shape((steps, SUB * TC, E), bf16), shape((steps, E, SUB * TC), bf16)),
        in_specs=[tile],
        out_specs=(rows_tile, cols_tile),
        compiler_params=params,
        cost_estimate=pl.CostEstimate(flops=10**9, bytes_accessed=10**7, transcendentals=0),
    )(centres)
    ut, all_labels, flags = pl.pallas_call(
        functools.partial(gather_kernel, n),
        out_shape=(
            shape((E, batch), bf16),
            shape((1, batch), jnp.int32),
            shape((local // FT, 128), jnp.int32),
        ),
        in_specs=[smem, vmem],
        out_specs=(vmem, vmem, vmem),
        compiler_params=params,
    )(where, got)

    height = 2 * n + EXTRA
    pt, payload, own_target, own = pl.pallas_call(
        forward_kernel,
        grid=(steps,),
        out_shape=(
            shape((SUB, local, batch), bf16),
            shape((parts, height, E), bf16),
            shape((8, batch), f32),
            shape((8, batch), f32),
        ),
        in_specs=[smem, smem, rows_tile, cols_tile, whole((E, batch)), whole((1, batch))],
        out_specs=(
            vmem,
            whole((parts, height, E)),
            whole((8, batch)),
            whole((8, batch)),
        ),
        scratch_shapes=[
            pltpu.VMEM((2, SUB * TC, BB), f32),
            pltpu.VMEM((8, batch), f32),
            pltpu.VMEM((E, batch), f32),
            pltpu.VMEM((E, batch), f32),
        ],
        compiler_params=params,
    )(where, flags, cb, cbt, ut, all_labels)

    got1 = lax.all_to_all(payload, "dp", 0, 0)
    second = pl.pallas_call(
        functools.partial(middle_kernel, n, blocks),
        out_shape=shape((others, 32, E), bf16),
        in_specs=[vmem],
        out_specs=vmem,
        compiler_params=params,
    )(got1)
    got2 = lax.all_to_all(second, "cls", 0, 0)
    loss, ust, fac, rows = pl.pallas_call(
        functools.partial(rows_kernel, m),
        out_shape=(
            shape((1, 1), f32),
            shape((E, batch), bf16),
            shape((8, batch), f32),
            shape((GROUP, m, E), bf16),
        ),
        in_specs=[smem, vmem, vmem, vmem, vmem, vmem],
        out_specs=(vmem, vmem, vmem, vmem),
        compiler_params=params,
    )(where, got2, embeddings, ut, own_target, own)
    groups = [list(range(g, g + GROUP)) for g in range(0, others, GROUP)]
    got3 = lax.all_to_all(rows, "cls", 0, 0, axis_index_groups=groups)
    grad_embeddings, grad_centres = pl.pallas_call(
        backward_kernel,
        grid=(steps,),
        out_shape=(shape((n, E), bf16), shape((SUB, local, E), bf16)),
        in_specs=[
            smem,
            smem,
            whole((8, batch)),
            whole((E, batch)),
            whole((1, batch)),
            whole((GROUP, m, E)),
            tile,
            vmem,
        ],
        out_specs=(whole((n, E)), tile),
        scratch_shapes=[pltpu.VMEM((SUB, TC, E), f32)],
        compiler_params=params,
    )(where, flags, fac, ust, all_labels, got3, centres, pt)
    return (loss.reshape(()), grad_embeddings, grad_centres)


def solution(mesh):
    return jax.shard_map(
        per_device,
        mesh=mesh,
        in_specs=(P("dp", None), P("dp"), P(None, ("dp", "cls"), None)),
        out_specs=(P(), P("dp", None), P(None, ("dp", "cls"), None)),
        check_vma=False,
    )
```

```python
import functools
import math

import jax
import jax.numpy as jnp
from jax import lax
from jax.experimental import pallas as pl
from jax.experimental.pallas import tpu as pltpu
from jax.sharding import PartitionSpec as P

norm_eps = 1e-06
logit_scale = 30.0
margin_value = 0.2
pool_temp = 0.1

LN2 = math.log(2.0)
A = 1.0 / (pool_temp * LN2)
L = logit_scale * pool_temp
MARGIN2 = logit_scale * margin_value / LN2
INV_LN2 = 1.0 / LN2
OUT_SCALE = logit_scale * LN2

SUB = 3
E = 256
TC = 512
BB = 256
FT = 256
FC = 64
FB = 128
RC = 16
AWAY = -1e4
EXTRA = 16
GROUP = 8

DIM0 = (((0,), (0,)), ((), ()))
DIM1 = (((1,), (1,)), ((), ()))

f32 = jnp.float32
bf16 = jnp.bfloat16


def split3(x):
    hi = x.astype(bf16)
    rest = x - hi.astype(f32)
    mid = rest.astype(bf16)
    lo = (rest - mid.astype(f32)).astype(bf16)
    return hi, mid, lo


def inv_norm(floats):
    mean = jnp.sum(floats * floats, axis=-1, keepdims=True) * (1.0 / E)
    return lax.rsqrt(E * (mean + norm_eps))


def send_kernel(slot_ref, emb_ref, lab_ref, out_ref):
    rows = emb_ref[...].astype(f32)
    unit = (rows * inv_norm(rows)).astype(bf16)
    n = rows.shape[0]
    labels = lab_ref[...]
    lane = lax.broadcasted_iota(jnp.int32, (1, E), 1)
    wide = jnp.concatenate([labels] * (E // n), axis=1)
    mine = (lane >= slot_ref[0]) & (lane < slot_ref[0] + n)
    wide = jnp.where(mine, wide, 0)
    row = lax.broadcasted_iota(jnp.int32, (16, E), 0)
    digit = jnp.where(row == 0, wide & 127, jnp.where(row == 1, (wide >> 7) & 127, wide >> 14))
    digit = jnp.where(row < 3, digit, 0).astype(f32).astype(bf16)
    for j in range(out_ref.shape[0]):
        out_ref[j, pl.ds(0, n), :] = unit
        out_ref[j, pl.ds(n, 16), :] = digit


def centre_kernel(cent_ref, cb_ref):
    for k in range(SUB):
        rows = cent_ref[k].astype(f32)
        unit = rows * inv_norm(rows)
        cb_ref[0, pl.ds(k * TC, TC), :] = unit.astype(bf16)


def gather_kernel(rows_own, where_ref, got_ref, ut_ref, lab_ref, flag_ref):
    parts = got_ref.shape[0]
    per = E // rows_own
    for q in range(parts // per):
        digits = jnp.zeros((16, E), f32)
        for j in range(per):
            digits += got_ref[q * per + j, pl.ds(rows_own, 16), :].astype(f32)
        lab = digits[0:1] + 128.0 * digits[1:2] + 16384.0 * digits[2:3]
        lab_ref[:, pl.ds(q * E, E)] = lab.astype(jnp.int32)
        block = jnp.concatenate(
            [got_ref[q * per + j, pl.ds(0, rows_own), :].astype(f32) for j in range(per)], axis=0
        )
        ut_ref[:, pl.ds(q * E, E)] = block.T.astype(bf16)
    words, width = flag_ref.shape
    batch = lab_ref.shape[1]
    tile = (lab_ref[...] - where_ref[0]) >> (FC.bit_length() - 1)
    lane = lax.broadcasted_iota(jnp.int32, (words, width), 1)
    row = lax.broadcasted_iota(jnp.int32, (words, batch), 0) * (FT // FC)
    flags = jnp.zeros((words, width), jnp.int32)
    for i in range(FT // FC):
        hits = (row + i == tile).astype(f32)
        for b in range(batch // FB):
            some = jnp.sum(hits[:, b * FB : (b + 1) * FB], axis=1, keepdims=True) > 0
            j = b % (BB // FB)
            bit = jnp.where(some, 1 << (i * (BB // FB) + j), 0)
            flags += jnp.where(lane == b // (BB // FB), bit, 0)
    flag_ref[...] = flags


def elementwise(c0, c1, c2):
    d1 = (c1 - c0) * A
    d2 = (c2 - c0) * A
    e1 = jnp.exp2(d1)
    e2 = jnp.exp2(d2)
    r = 1.0 / (1.0 + e1 + e2)
    z = (e1 * d1 + e2 * d2) * r
    power = c0 * (L * A) + z * L
    shift = INV_LN2 - z
    return e1, e2, d1, d2, r, power, shift


def forward_kernel(
    first_ref, flag_ref, cb_ref, ut_ref, lab_ref,
    pt_ref, out_ref, target, own_ref, xs, sums, g1, g2,
):
    step = pl.program_id(0)
    steps = pl.num_programs(0)
    batch = ut_ref.shape[1]

    @pl.when(step == 0)
    def _():
        sums[...] = jnp.zeros_like(sums)
        target[...] = jnp.zeros_like(target)
        own_ref[...] = jnp.zeros_like(own_ref)
        g1[...] = jnp.zeros_like(g1)
        g2[...] = jnp.zeros_like(g2)

    first = first_ref[0] + step * TC
    base = pl.multiple_of(step * TC, TC)

    def block(b):
        cols = pl.ds(b * BB, BB)
        xs[b % 2] = jnp.dot(cb_ref[0], ut_ref[:, cols], preferred_element_type=f32)

    def set_labels_apart(b, h, word):
        per = BB // FB

        def piece(i, carry):
            @pl.when(((word >> i) & 1) > 0)
            def _():
                down = pl.multiple_of((i // per) * FC, FC) + h * FT
                over = pl.multiple_of((i % per) * FB, FB)
                here = pl.ds(over, FB)
                cols = pl.ds(pl.multiple_of(over + b * BB, FB), FB)
                row = lax.broadcasted_iota(jnp.int32, (FC, FB), 0) + down
                hit = row == lab_ref[:, cols] - first
                known = jnp.sum(jnp.where(hit, 1.0, 0.0), axis=0, keepdims=True) > 0
                x = []
                for k in range(SUB):
                    rows = pl.ds(pl.multiple_of(down + k * TC, FC), FC)
                    v = xs[b % 2, rows, here]
                    x.append(jnp.sum(jnp.where(hit, v, 0.0), axis=0, keepdims=True))
                    xs[b % 2, rows, here] = jnp.where(hit, AWAY, v)
                e1, e2, d1, d2, r, power, shift = elementwise(*x)
                power = power - MARGIN2
                target[0:1, cols] += jnp.where(known, power, 0.0)
                sums[0:1, cols] += jnp.where(known, jnp.exp2(power), 0.0)
                p = (r * shift, (r * e1) * (d1 + shift), (r * e2) * (d2 + shift))
                add = jnp.zeros((FB, E), f32)
                for k in range(SUB):
                    own_ref[k : k + 1, cols] += jnp.where(known, p[k], 0.0)
                    own = jnp.where(hit, p[k], 0.0).astype(bf16)
                    cb = cb_ref[0, pl.ds(pl.multiple_of(down + k * TC, FC), FC), :]
                    add += lax.dot_general(own, cb, DIM0, preferred_element_type=f32)
                g2[cols, :] += add

            return carry

        lax.fori_loop(0, (FT // FC) * per, piece, 0)

    def terms(b):
        cols = pl.ds(b * BB, BB)
        total = jnp.zeros((8, BB), f32)
        for c in range(TC // RC):
            x = [xs[b % 2, pl.ds(k * TC + c * RC, RC), :] for k in range(SUB)]
            e1, e2, d1, d2, r, power, shift = elementwise(*x)
            ex = jnp.exp2(power)
            total += ex[0:8] + ex[8:16]
            g = ex * r
            p = (g * shift, (g * e1) * (d1 + shift), (g * e2) * (d2 + shift))
            for k in range(SUB):
                pt_ref[k, pl.ds(base + c * RC, RC), cols] = p[k].astype(bf16)
        sums[:, cols] += total

    def rows_sum(b):
        cols = pl.ds(b * BB, BB)
        p = jnp.concatenate([pt_ref[k, pl.ds(base, TC), cols] for k in range(SUB)], axis=0)
        g1[:, cols] += lax.dot_general(cb_ref[0], p, DIM0, preferred_element_type=f32)

    block(0)
    for b in range(batch // BB):
        for h in range(TC // FT):
            word = flag_ref[step * (TC // FT) + h, b]
            pl.when(word > 0)(functools.partial(set_labels_apart, b, h, word))
        if (b + 1) * BB < batch:
            block(b + 1)
        terms(b)
        rows_sum(b)

    @pl.when(step == steps - 1)
    def _():
        parts = out_ref.shape[0]
        n = batch // parts
        per = E // n
        blocks = batch // E
        tot = jnp.sum(sums[...], axis=0, keepdims=True)
        tgt = jnp.sum(target[...], axis=0, keepdims=True)
        all_targets = jnp.sum(tgt, axis=1, keepdims=True)
        totals = jnp.concatenate([tot[:, q * E : (q + 1) * E] for q in range(blocks)], axis=0)
        for q in range(blocks):
            cols = slice(q * E, (q + 1) * E)
            a = g1[:, cols].T.astype(bf16)
            o = g2[q * E : (q + 1) * E, :].astype(bf16)
            extra = pack_extra(totals, tgt[:, cols], all_targets).astype(bf16)
            for j in range(per):
                out_ref[q * per + j, pl.ds(0, n), :] = a[j * n : (j + 1) * n]
                out_ref[q * per + j, pl.ds(n, n), :] = o[j * n : (j + 1) * n]
                out_ref[q * per + j, pl.ds(2 * n, EXTRA), :] = extra


def pack_extra(totals, target, all_targets):
    lane = lax.broadcasted_iota(jnp.int32, (1, E), 1)
    hi, mid, lo = split3(all_targets)
    tail = jnp.where(lane == 0, hi.astype(f32), jnp.where(lane == 1, mid.astype(f32), 0.0))
    tail = jnp.where(lane == 2, lo.astype(f32), tail)
    values = [v.astype(f32) for v in split3(totals)] + [v.astype(f32) for v in split3(target)]
    pad = EXTRA - 3 * totals.shape[0] - 4
    return jnp.concatenate(values + [tail] + [jnp.zeros((pad, E), f32)] * (pad > 0), axis=0)


def unpack_extra(extra, blocks):
    totals = extra[0:blocks] + extra[blocks : 2 * blocks] + extra[2 * blocks : 3 * blocks]
    m = 3 * blocks
    target = extra[m : m + 1] + extra[m + 1 : m + 2] + extra[m + 2 : m + 3]
    all_targets = jnp.sum(extra[m + 3 : m + 4], axis=1, keepdims=True)
    return totals, target, all_targets


def summed(got_ref):
    acc = got_ref[0].astype(f32)
    for j in range(1, got_ref.shape[0]):
        acc += got_ref[j].astype(f32)
    return acc


def middle_kernel(n, blocks, got_ref, out_ref):
    acc = summed(got_ref)
    extra = pack_extra(*unpack_extra(acc[2 * n :], blocks))
    others, height = out_ref.shape[0], out_ref.shape[1]
    m = n // GROUP
    pad = jnp.zeros((height - 2 * m - EXTRA, E), f32)
    for j in range(others):
        at = (j % GROUP) * m
        one = acc[at : at + m]
        two = acc[n + at : n + at + m]
        out_ref[j] = jnp.concatenate([one, two, extra] + [pad] * (pad.shape[0] > 0), axis=0).astype(bf16)


def rows_kernel(
    m, where_ref, got_ref, emb_ref, ut_ref, target_ref, own_ref,
    loss_ref, ust_ref, fac_ref, rows_ref,
):
    batch = ut_ref.shape[1]
    blocks = batch // E
    n = emb_ref.shape[0]
    acc = summed(got_ref)
    totals, target, all_targets = unpack_extra(acc[2 * m : 2 * m + EXTRA], blocks)
    tot = jnp.concatenate([totals[q : q + 1] for q in range(blocks)], axis=1)
    logs = jnp.sum(jnp.log(tot), axis=1, keepdims=True) - all_targets * LN2
    loss_ref[...] = logs * (1.0 / batch)
    inv = OUT_SCALE / tot
    ust_ref[...] = (ut_ref[...].astype(f32) * inv).astype(bf16)
    own_target = jnp.sum(target_ref[...], axis=0, keepdims=True)
    fac_ref[...] = own_ref[...] * (jnp.exp2(own_target) - tot)
    lane = lax.broadcasted_iota(jnp.int32, (m, batch), 1)
    row = lax.broadcasted_iota(jnp.int32, (m, batch), 0)
    inv_col = jnp.sum(jnp.where(lane == row + where_ref[1], inv, 0.0), axis=1, keepdims=True)
    lane = lax.broadcasted_iota(jnp.int32, (m, E), 1)
    row = lax.broadcasted_iota(jnp.int32, (m, E), 0)
    mine = lane == row + where_ref[2]
    t = jnp.sum(jnp.where(mine, target, 0.0), axis=1, keepdims=True)
    g = acc[0:m] * inv_col + acc[m : 2 * m] * (jnp.exp2(t) * inv_col - OUT_SCALE)
    lane = lax.broadcasted_iota(jnp.int32, (m, n), 1)
    row = lax.broadcasted_iota(jnp.int32, (m, n), 0)
    pick = jnp.where(lane == row + where_ref[3], 1.0, 0.0).astype(bf16)
    rows = jnp.dot(pick, emb_ref[...], preferred_element_type=f32)
    r = inv_norm(rows)
    unit = rows * r
    g = (g - unit * jnp.sum(unit * g, axis=1, keepdims=True)) * r
    for j in range(rows_ref.shape[0]):
        rows_ref[j] = g.astype(bf16)


def backward_kernel(
    first_ref, flag_ref, fac_ref, ust_ref, lab_ref, got_ref, cent_ref, pt_ref, ge_ref, gc_ref
):
    step = pl.program_id(0)
    batch = ust_ref.shape[1]
    first = first_ref[0] + step * TC
    base = pl.multiple_of(step * TC, TC)

    @pl.when(step == 0)
    def _():
        parts = [got_ref[j].astype(f32) for j in range(got_ref.shape[0])]
        ge_ref[...] = jnp.concatenate(parts, axis=0).astype(bf16)

    def finish(rows, g):
        rows = rows.astype(f32)
        r = inv_norm(rows)
        unit = rows * r
        g = (g - unit * jnp.sum(unit * g, axis=1, keepdims=True)) * r
        return g.astype(bf16)

    for k in range(SUB):
        p = pt_ref[k, pl.ds(base, TC), :]
        g = lax.dot_general(p, ust_ref[...], DIM1, preferred_element_type=f32)
        gc_ref[k] = finish(cent_ref[k], g)

    per = BB // FB
    for h in range(TC // FT):
        words = [flag_ref[step * (TC // FT) + h, b] for b in range(batch // BB)]
        word = functools.reduce(lambda x, y: x | y, words)

        def piece(i, carry, word=word, h=h):
            @pl.when(((word >> (i * per)) & ((1 << per) - 1)) > 0)
            def _():
                down = pl.multiple_of(i * FC + h * FT, FC)
                row = lax.broadcasted_iota(jnp.int32, (FC, batch), 0) + down
                hit = row == lab_ref[...] - first
                p = []
                for k in range(SUB):
                    v = pt_ref[k, pl.ds(pl.multiple_of(base + down, FC), FC), :].astype(f32)
                    p.append(jnp.where(hit, fac_ref[k : k + 1, :], v).astype(bf16))
                p = jnp.concatenate(p, axis=0)
                g = lax.dot_general(p, ust_ref[...], DIM1, preferred_element_type=f32)
                for k in range(SUB):
                    rows = pl.ds(down, FC)
                    gc_ref[k, rows, :] = finish(
                        cent_ref[k, rows, :], g[k * FC : (k + 1) * FC]
                    )

            return carry

        @pl.when(word > 0)
        def _(piece=piece):
            lax.fori_loop(0, FT // FC, piece, 0)


def per_device(embeddings, labels, centres):
    n = embeddings.shape[0]
    parts = lax.axis_size("dp")
    others = lax.axis_size("cls")
    batch = n * parts
    blocks = batch // E
    local = centres.shape[1]
    steps = local // TC
    m = n // GROUP
    dp = lax.axis_index("dp")
    cls = lax.axis_index("cls")
    first = (dp * others + cls) * local
    slot = (dp & (E // n - 1)) * n
    at = (cls & (GROUP - 1)) * m
    where = jnp.stack([first, dp * n + at, slot + at, at]).astype(jnp.int32)
    smem = pl.BlockSpec(memory_space=pltpu.SMEM)
    vmem = pl.BlockSpec(memory_space=pltpu.VMEM)
    params = pltpu.CompilerParams(vmem_limit_bytes=24 * 1024 * 1024)
    shape = jax.ShapeDtypeStruct

    sent = pl.pallas_call(
        send_kernel,
        out_shape=shape((parts, n + 16, E), bf16),
        in_specs=[smem, vmem, vmem],
        out_specs=vmem,
    )(slot.astype(jnp.int32).reshape(1), embeddings, labels.reshape(1, n))
    got = lax.all_to_all(sent, "dp", 0, 0)
    tile = pl.BlockSpec((SUB, TC, E), lambda i: (0, i, 0))
    rows_tile = pl.BlockSpec((1, SUB * TC, E), lambda i: (i, 0, 0))
    cb = pl.pallas_call(
        centre_kernel,
        grid=(steps,),
        out_shape=shape((steps, SUB * TC, E), bf16),
        in_specs=[tile],
        out_specs=rows_tile,
        compiler_params=params,
        cost_estimate=pl.CostEstimate(flops=10**9, bytes_accessed=10**7, transcendentals=0),
    )(centres)
    ut, all_labels, flags = pl.pallas_call(
        functools.partial(gather_kernel, n),
        out_shape=(
            shape((E, batch), bf16),
            shape((1, batch), jnp.int32),
            shape((local // FT, 128), jnp.int32),
        ),
        in_specs=[smem, vmem],
        out_specs=(vmem, vmem, vmem),
        compiler_params=params,
    )(where, got)

    height = 2 * n + EXTRA
    pt, payload, own_target, own = pl.pallas_call(
        forward_kernel,
        grid=(steps,),
        out_shape=(
            shape((SUB, local, batch), bf16),
            shape((parts, height, E), bf16),
            shape((8, batch), f32),
            shape((8, batch), f32),
        ),
        in_specs=[smem, smem, rows_tile, vmem, vmem],
        out_specs=(vmem, vmem, vmem, vmem),
        scratch_shapes=[
            pltpu.VMEM((2, SUB * TC, BB), f32),
            pltpu.VMEM((8, batch), f32),
            pltpu.VMEM((E, batch), f32),
            pltpu.VMEM((batch, E), f32),
        ],
        compiler_params=params,
    )(where, flags, cb, ut, all_labels)

    got1 = lax.all_to_all(payload, "dp", 0, 0)
    second = pl.pallas_call(
        functools.partial(middle_kernel, n, blocks),
        out_shape=shape((others, 32, E), bf16),
        in_specs=[vmem],
        out_specs=vmem,
        compiler_params=params,
    )(got1)
    got2 = lax.all_to_all(second, "cls", 0, 0)
    loss, ust, fac, rows = pl.pallas_call(
        functools.partial(rows_kernel, m),
        out_shape=(
            shape((1, 1), f32),
            shape((E, batch), bf16),
            shape((8, batch), f32),
            shape((GROUP, m, E), bf16),
        ),
        in_specs=[smem, vmem, vmem, vmem, vmem, vmem],
        out_specs=(vmem, vmem, vmem, vmem),
        compiler_params=params,
    )(where, got2, embeddings, ut, own_target, own)
    groups = [list(range(g, g + GROUP)) for g in range(0, others, GROUP)]
    got3 = lax.all_to_all(rows, "cls", 0, 0, axis_index_groups=groups)
    grad_embeddings, grad_centres = pl.pallas_call(
        backward_kernel,
        grid=(steps,),
        out_shape=(shape((n, E), bf16), shape((SUB, local, E), bf16)),
        in_specs=[
            smem,
            smem,
            vmem,
            vmem,
            vmem,
            vmem,
            tile,
            vmem,
        ],
        out_specs=(vmem, tile),
        compiler_params=params,
    )(where, flags, fac, ust, all_labels, got3, centres, pt)
    return (loss.reshape(()), grad_embeddings, grad_centres)


def solution(mesh):
    return jax.shard_map(
        per_device,
        mesh=mesh,
        in_specs=(P("dp", None), P("dp"), P(None, ("dp", "cls"), None)),
        out_specs=(P(), P("dp", None), P(None, ("dp", "cls"), None)),
        check_vma=False,
    )
```

```python
import functools
import math

import jax
import jax.numpy as jnp
from jax import lax
from jax.experimental import pallas as pl
from jax.experimental.pallas import tpu as pltpu
from jax.sharding import PartitionSpec as P

norm_eps = 1e-06
logit_scale = 30.0
margin_value = 0.2
pool_temp = 0.1

LN2 = math.log(2.0)
A = 1.0 / (pool_temp * LN2)
L = logit_scale * pool_temp
MARGIN2 = logit_scale * margin_value / LN2
INV_LN2 = 1.0 / LN2
OUT_SCALE = logit_scale * LN2

SUB = 3
E = 256
TC = 512
BB = 256
FT = 256
FC = 64
FB = 128
RC = 16
AWAY = -1e4
EXTRA = 16
GROUP = 8

DIM0 = (((0,), (0,)), ((), ()))
DIM1 = (((1,), (1,)), ((), ()))

f32 = jnp.float32
bf16 = jnp.bfloat16


def split3(x):
    hi = x.astype(bf16)
    rest = x - hi.astype(f32)
    mid = rest.astype(bf16)
    lo = (rest - mid.astype(f32)).astype(bf16)
    return hi, mid, lo


def inv_norm(floats):
    mean = jnp.sum(floats * floats, axis=-1, keepdims=True) * (1.0 / E)
    return lax.rsqrt(E * (mean + norm_eps))


def send_kernel(slot_ref, emb_ref, lab_ref, out_ref):
    rows = emb_ref[...].astype(f32)
    unit = (rows * inv_norm(rows)).astype(bf16)
    n = rows.shape[0]
    labels = lab_ref[...]
    lane = lax.broadcasted_iota(jnp.int32, (1, E), 1)
    wide = jnp.concatenate([labels] * (E // n), axis=1)
    mine = (lane >= slot_ref[0]) & (lane < slot_ref[0] + n)
    wide = jnp.where(mine, wide, 0)
    row = lax.broadcasted_iota(jnp.int32, (16, E), 0)
    digit = jnp.where(row == 0, wide & 127, jnp.where(row == 1, (wide >> 7) & 127, wide >> 14))
    digit = jnp.where(row < 3, digit, 0).astype(f32).astype(bf16)
    for j in range(out_ref.shape[0]):
        out_ref[j, pl.ds(0, n), :] = unit
        out_ref[j, pl.ds(n, 16), :] = digit


def centre_kernel(cent_ref, cb_ref):
    for k in range(SUB):
        rows = cent_ref[k].astype(f32)
        unit = rows * inv_norm(rows)
        cb_ref[0, pl.ds(k * TC, TC), :] = unit.astype(bf16)


def gather_kernel(rows_own, where_ref, got_ref, ut_ref, lab_ref, flag_ref):
    parts = got_ref.shape[0]
    per = E // rows_own
    for q in range(parts // per):
        digits = jnp.zeros((16, E), f32)
        for j in range(per):
            digits += got_ref[q * per + j, pl.ds(rows_own, 16), :].astype(f32)
        lab = digits[0:1] + 128.0 * digits[1:2] + 16384.0 * digits[2:3]
        lab_ref[:, pl.ds(q * E, E)] = lab.astype(jnp.int32)
        block = jnp.concatenate(
            [got_ref[q * per + j, pl.ds(0, rows_own), :].astype(f32) for j in range(per)], axis=0
        )
        ut_ref[:, pl.ds(q * E, E)] = block.T.astype(bf16)
    words, width = flag_ref.shape
    batch = lab_ref.shape[1]
    tile = (lab_ref[...] - where_ref[0]) >> (FC.bit_length() - 1)
    lane = lax.broadcasted_iota(jnp.int32, (words, width), 1)
    row = lax.broadcasted_iota(jnp.int32, (words, batch), 0) * (FT // FC)
    flags = jnp.zeros((words, width), jnp.int32)
    for i in range(FT // FC):
        hits = (row + i == tile).astype(f32)
        for b in range(batch // FB):
            some = jnp.sum(hits[:, b * FB : (b + 1) * FB], axis=1, keepdims=True) > 0
            j = b % (BB // FB)
            bit = jnp.where(some, 1 << (i * (BB // FB) + j), 0)
            flags += jnp.where(lane == b // (BB // FB), bit, 0)
    flag_ref[...] = flags


def elementwise(c0, c1, c2):
    d1 = (c1 - c0) * A
    d2 = (c2 - c0) * A
    e1 = jnp.exp2(d1)
    e2 = jnp.exp2(d2)
    r = 1.0 / (1.0 + e1 + e2)
    z = (e1 * d1 + e2 * d2) * r
    power = c0 * (L * A) + z * L
    shift = INV_LN2 - z
    return e1, e2, d1, d2, r, power, shift


def forward_kernel(
    first_ref, flag_ref, cb_ref, next_ref, ut_ref, lab_ref,
    pt_ref, out_ref, target, own_ref, xs, sums, g1, g2,
):
    step = pl.program_id(0)
    steps = pl.num_programs(0)
    batch = ut_ref.shape[1]

    @pl.when(step == 0)
    def _():
        sums[...] = jnp.zeros_like(sums)
        target[...] = jnp.zeros_like(target)
        own_ref[...] = jnp.zeros_like(own_ref)
        g1[...] = jnp.zeros_like(g1)
        g2[...] = jnp.zeros_like(g2)

    first = first_ref[0] + step * TC
    tile_ref = pt_ref.at[step]

    def block(ref, b):
        cols = pl.ds(b * BB, BB)
        xs[b] = jnp.dot(ref[0], ut_ref[:, cols], preferred_element_type=f32)

    def set_labels_apart(b, h, word):
        per = BB // FB

        def piece(i, carry):
            @pl.when(((word >> i) & 1) > 0)
            def _():
                down = pl.multiple_of((i // per) * FC, FC) + h * FT
                over = pl.multiple_of((i % per) * FB, FB)
                here = pl.ds(over, FB)
                cols = pl.ds(pl.multiple_of(over + b * BB, FB), FB)
                row = lax.broadcasted_iota(jnp.int32, (FC, FB), 0) + down
                hit = row == lab_ref[:, cols] - first
                known = jnp.sum(jnp.where(hit, 1.0, 0.0), axis=0, keepdims=True) > 0
                x = []
                for k in range(SUB):
                    rows = pl.ds(pl.multiple_of(down + k * TC, FC), FC)
                    v = xs[b, rows, here]
                    x.append(jnp.sum(jnp.where(hit, v, 0.0), axis=0, keepdims=True))
                    xs[b, rows, here] = jnp.where(hit, AWAY, v)
                e1, e2, d1, d2, r, power, shift = elementwise(*x)
                power = power - MARGIN2
                target[0:1, cols] += jnp.where(known, power, 0.0)
                sums[0:1, cols] += jnp.where(known, jnp.exp2(power), 0.0)
                p = (r * shift, (r * e1) * (d1 + shift), (r * e2) * (d2 + shift))
                add = jnp.zeros((FB, E), f32)
                for k in range(SUB):
                    own_ref[k : k + 1, cols] += jnp.where(known, p[k], 0.0)
                    own = jnp.where(hit, p[k], 0.0).astype(bf16)
                    cb = cb_ref[0, pl.ds(pl.multiple_of(down + k * TC, FC), FC), :]
                    add += lax.dot_general(own, cb, DIM0, preferred_element_type=f32)
                g2[cols, :] += add

            return carry

        lax.fori_loop(0, (FT // FC) * per, piece, 0)

    def terms(b):
        cols = pl.ds(b * BB, BB)
        total = jnp.zeros((8, BB), f32)
        for c in range(TC // RC):
            x = [xs[b, pl.ds(k * TC + c * RC, RC), :] for k in range(SUB)]
            e1, e2, d1, d2, r, power, shift = elementwise(*x)
            ex = jnp.exp2(power)
            total += ex[0:8] + ex[8:16]
            g = ex * r
            p = (g * shift, (g * e1) * (d1 + shift), (g * e2) * (d2 + shift))
            for k in range(SUB):
                tile_ref[k, pl.ds(c * RC, RC), cols] = p[k].astype(bf16)
        sums[:, cols] += total

    def rows_sum(b):
        cols = pl.ds(b * BB, BB)
        p = jnp.concatenate([tile_ref[k, :, cols] for k in range(SUB)], axis=0)
        g1[:, cols] += lax.dot_general(cb_ref[0], p, DIM0, preferred_element_type=f32)

    @pl.when(step == 0)
    def _():
        for b in range(batch // BB):
            block(cb_ref, b)

    words = [
        (b, h, flag_ref[step * (TC // FT) + h, b])
        for b in range(batch // BB)
        for h in range(TC // FT)
    ]

    @pl.when(functools.reduce(lambda x, y: x | y, [w for _, _, w in words]) > 0)
    def _():
        for b, h, word in words:
            pl.when(word > 0)(functools.partial(set_labels_apart, b, h, word))

    for b in range(batch // BB):
        terms(b)
        block(next_ref, b)
        rows_sum(b)

    @pl.when(step == steps - 1)
    def _():
        parts = out_ref.shape[0]
        n = batch // parts
        per = E // n
        blocks = batch // E
        tot = jnp.sum(sums[...], axis=0, keepdims=True)
        tgt = jnp.sum(target[...], axis=0, keepdims=True)
        all_targets = jnp.sum(tgt, axis=1, keepdims=True)
        totals = jnp.concatenate([tot[:, q * E : (q + 1) * E] for q in range(blocks)], axis=0)
        for q in range(blocks):
            cols = slice(q * E, (q + 1) * E)
            a = g1[:, cols].T.astype(bf16)
            o = g2[q * E : (q + 1) * E, :].astype(bf16)
            extra = pack_extra(totals, tgt[:, cols], all_targets).astype(bf16)
            for j in range(per):
                out_ref[q * per + j, pl.ds(0, n), :] = a[j * n : (j + 1) * n]
                out_ref[q * per + j, pl.ds(n, n), :] = o[j * n : (j + 1) * n]
                out_ref[q * per + j, pl.ds(2 * n, EXTRA), :] = extra


def pack_extra(totals, target, all_targets):
    lane = lax.broadcasted_iota(jnp.int32, (1, E), 1)
    hi, mid, lo = split3(all_targets)
    tail = jnp.where(lane == 0, hi.astype(f32), jnp.where(lane == 1, mid.astype(f32), 0.0))
    tail = jnp.where(lane == 2, lo.astype(f32), tail)
    values = [v.astype(f32) for v in split3(totals)] + [v.astype(f32) for v in split3(target)]
    pad = EXTRA - 3 * totals.shape[0] - 4
    return jnp.concatenate(values + [tail] + [jnp.zeros((pad, E), f32)] * (pad > 0), axis=0)


def unpack_extra(extra, blocks):
    totals = extra[0:blocks] + extra[blocks : 2 * blocks] + extra[2 * blocks : 3 * blocks]
    m = 3 * blocks
    target = extra[m : m + 1] + extra[m + 1 : m + 2] + extra[m + 2 : m + 3]
    all_targets = jnp.sum(extra[m + 3 : m + 4], axis=1, keepdims=True)
    return totals, target, all_targets


def summed(got_ref):
    acc = got_ref[0].astype(f32)
    for j in range(1, got_ref.shape[0]):
        acc += got_ref[j].astype(f32)
    return acc


def middle_kernel(n, blocks, got_ref, out_ref):
    acc = summed(got_ref)
    extra = pack_extra(*unpack_extra(acc[2 * n :], blocks))
    others, height = out_ref.shape[0], out_ref.shape[1]
    m = n // GROUP
    pad = jnp.zeros((height - 2 * m - EXTRA, E), f32)
    for j in range(others):
        at = (j % GROUP) * m
        one = acc[at : at + m]
        two = acc[n + at : n + at + m]
        out_ref[j] = jnp.concatenate([one, two, extra] + [pad] * (pad.shape[0] > 0), axis=0).astype(bf16)


def rows_kernel(
    m, where_ref, got_ref, emb_ref, ut_ref, target_ref, own_ref,
    loss_ref, ust_ref, fac_ref, rows_ref,
):
    batch = ut_ref.shape[1]
    blocks = batch // E
    n = emb_ref.shape[0]
    acc = summed(got_ref)
    totals, target, all_targets = unpack_extra(acc[2 * m : 2 * m + EXTRA], blocks)
    tot = jnp.concatenate([totals[q : q + 1] for q in range(blocks)], axis=1)
    logs = jnp.sum(jnp.log(tot), axis=1, keepdims=True) - all_targets * LN2
    loss_ref[...] = logs * (1.0 / batch)
    inv = OUT_SCALE / tot
    ust_ref[...] = (ut_ref[...].astype(f32) * inv).astype(bf16)
    own_target = jnp.sum(target_ref[...], axis=0, keepdims=True)
    fac_ref[...] = own_ref[...] * (jnp.exp2(own_target) - tot)
    lane = lax.broadcasted_iota(jnp.int32, (m, batch), 1)
    row = lax.broadcasted_iota(jnp.int32, (m, batch), 0)
    inv_col = jnp.sum(jnp.where(lane == row + where_ref[1], inv, 0.0), axis=1, keepdims=True)
    lane = lax.broadcasted_iota(jnp.int32, (m, E), 1)
    row = lax.broadcasted_iota(jnp.int32, (m, E), 0)
    mine = lane == row + where_ref[2]
    t = jnp.sum(jnp.where(mine, target, 0.0), axis=1, keepdims=True)
    g = acc[0:m] * inv_col + acc[m : 2 * m] * (jnp.exp2(t) * inv_col - OUT_SCALE)
    lane = lax.broadcasted_iota(jnp.int32, (m, n), 1)
    row = lax.broadcasted_iota(jnp.int32, (m, n), 0)
    pick = jnp.where(lane == row + where_ref[3], 1.0, 0.0).astype(bf16)
    rows = jnp.dot(pick, emb_ref[...], preferred_element_type=f32)
    r = inv_norm(rows)
    unit = rows * r
    g = (g - unit * jnp.sum(unit * g, axis=1, keepdims=True)) * r
    for j in range(rows_ref.shape[0]):
        rows_ref[j] = g.astype(bf16)


def backward_kernel(
    first_ref, flag_ref, fac_ref, ust_ref, lab_ref, got_ref, cent_ref, pt_ref, ge_ref, gc_ref
):
    step = pl.program_id(0)
    batch = ust_ref.shape[1]
    first = first_ref[0] + step * TC

    @pl.when(step == 0)
    def _():
        parts = [got_ref[j].astype(f32) for j in range(got_ref.shape[0])]
        ge_ref[...] = jnp.concatenate(parts, axis=0).astype(bf16)

    def finish(rows, g):
        rows = rows.astype(f32)
        r = inv_norm(rows)
        unit = rows * r
        g = (g - unit * jnp.sum(unit * g, axis=1, keepdims=True)) * r
        return g.astype(bf16)

    for k in range(SUB):
        p = pt_ref[step, k]
        g = lax.dot_general(p, ust_ref[...], DIM1, preferred_element_type=f32)
        gc_ref[k] = finish(cent_ref[k], g)

    per = BB // FB
    for h in range(TC // FT):
        words = [flag_ref[step * (TC // FT) + h, b] for b in range(batch // BB)]
        word = functools.reduce(lambda x, y: x | y, words)

        def piece(i, carry, word=word, h=h):
            @pl.when(((word >> (i * per)) & ((1 << per) - 1)) > 0)
            def _():
                down = pl.multiple_of(i * FC + h * FT, FC)
                row = lax.broadcasted_iota(jnp.int32, (FC, batch), 0) + down
                hit = row == lab_ref[...] - first
                p = []
                for k in range(SUB):
                    v = pt_ref[step, k, pl.ds(down, FC), :].astype(f32)
                    p.append(jnp.where(hit, fac_ref[k : k + 1, :], v).astype(bf16))
                p = jnp.concatenate(p, axis=0)
                g = lax.dot_general(p, ust_ref[...], DIM1, preferred_element_type=f32)
                for k in range(SUB):
                    rows = pl.ds(down, FC)
                    gc_ref[k, rows, :] = finish(
                        cent_ref[k, rows, :], g[k * FC : (k + 1) * FC]
                    )

            return carry

        @pl.when(word > 0)
        def _(piece=piece):
            lax.fori_loop(0, FT // FC, piece, 0)


def per_device(embeddings, labels, centres):
    n = embeddings.shape[0]
    parts = lax.axis_size("dp")
    others = lax.axis_size("cls")
    batch = n * parts
    blocks = batch // E
    local = centres.shape[1]
    steps = local // TC
    m = n // GROUP
    dp = lax.axis_index("dp")
    cls = lax.axis_index("cls")
    first = (dp * others + cls) * local
    slot = (dp & (E // n - 1)) * n
    at = (cls & (GROUP - 1)) * m
    where = jnp.stack([first, dp * n + at, slot + at, at]).astype(jnp.int32)
    smem = pl.BlockSpec(memory_space=pltpu.SMEM)
    vmem = pl.BlockSpec(memory_space=pltpu.VMEM)
    params = pltpu.CompilerParams(vmem_limit_bytes=24 * 1024 * 1024)
    shape = jax.ShapeDtypeStruct

    sent = pl.pallas_call(
        send_kernel,
        out_shape=shape((parts, n + 16, E), bf16),
        in_specs=[smem, vmem, vmem],
        out_specs=vmem,
    )(slot.astype(jnp.int32).reshape(1), embeddings, labels.reshape(1, n))
    got = lax.all_to_all(sent, "dp", 0, 0)
    tile = pl.BlockSpec((SUB, TC, E), lambda i: (0, i, 0))
    rows_tile = pl.BlockSpec((1, SUB * TC, E), lambda i: (i, 0, 0))
    next_tile = pl.BlockSpec((1, SUB * TC, E), lambda i: (jnp.minimum(i + 1, steps - 1), 0, 0))
    cb = pl.pallas_call(
        centre_kernel,
        grid=(steps,),
        out_shape=shape((steps, SUB * TC, E), bf16),
        in_specs=[tile],
        out_specs=rows_tile,
        compiler_params=params,
        cost_estimate=pl.CostEstimate(flops=10**9, bytes_accessed=10**7, transcendentals=0),
    )(centres)
    ut, all_labels, flags = pl.pallas_call(
        functools.partial(gather_kernel, n),
        out_shape=(
            shape((E, batch), bf16),
            shape((1, batch), jnp.int32),
            shape((local // FT, 128), jnp.int32),
        ),
        in_specs=[smem, vmem],
        out_specs=(vmem, vmem, vmem),
        compiler_params=params,
    )(where, got)

    height = 2 * n + EXTRA
    pt, payload, own_target, own = pl.pallas_call(
        forward_kernel,
        grid=(steps,),
        out_shape=(
            shape((steps, SUB, TC, batch), bf16),
            shape((parts, height, E), bf16),
            shape((8, batch), f32),
            shape((8, batch), f32),
        ),
        in_specs=[smem, smem, rows_tile, next_tile, vmem, vmem],
        out_specs=(vmem, vmem, vmem, vmem),
        scratch_shapes=[
            pltpu.VMEM((batch // BB, SUB * TC, BB), f32),
            pltpu.VMEM((8, batch), f32),
            pltpu.VMEM((E, batch), f32),
            pltpu.VMEM((batch, E), f32),
        ],
        compiler_params=params,
    )(where, flags, cb, cb, ut, all_labels)

    got1 = lax.all_to_all(payload, "dp", 0, 0)
    second = pl.pallas_call(
        functools.partial(middle_kernel, n, blocks),
        out_shape=shape((others, 32, E), bf16),
        in_specs=[vmem],
        out_specs=vmem,
        compiler_params=params,
    )(got1)
    got2 = lax.all_to_all(second, "cls", 0, 0)
    loss, ust, fac, rows = pl.pallas_call(
        functools.partial(rows_kernel, m),
        out_shape=(
            shape((1, 1), f32),
            shape((E, batch), bf16),
            shape((8, batch), f32),
            shape((GROUP, m, E), bf16),
        ),
        in_specs=[smem, vmem, vmem, vmem, vmem, vmem],
        out_specs=(vmem, vmem, vmem, vmem),
        compiler_params=params,
    )(where, got2, embeddings, ut, own_target, own)
    groups = [list(range(g, g + GROUP)) for g in range(0, others, GROUP)]
    got3 = lax.all_to_all(rows, "cls", 0, 0, axis_index_groups=groups)
    grad_embeddings, grad_centres = pl.pallas_call(
        backward_kernel,
        grid=(steps,),
        out_shape=(shape((n, E), bf16), shape((SUB, local, E), bf16)),
        in_specs=[
            smem,
            smem,
            vmem,
            vmem,
            vmem,
            vmem,
            tile,
            vmem,
        ],
        out_specs=(vmem, tile),
        compiler_params=params,
    )(where, flags, fac, ust, all_labels, got3, centres, pt)
    return (loss.reshape(()), grad_embeddings, grad_centres)


def solution(mesh):
    return jax.shard_map(
        per_device,
        mesh=mesh,
        in_specs=(P("dp", None), P("dp"), P(None, ("dp", "cls"), None)),
        out_specs=(P(), P("dp", None), P(None, ("dp", "cls"), None)),
        check_vma=False,
    )
```

```python
import functools
import math

import jax
import jax.numpy as jnp
from jax import lax
from jax.experimental import pallas as pl
from jax.experimental.pallas import tpu as pltpu
from jax.sharding import PartitionSpec as P

norm_eps = 1e-06
logit_scale = 30.0
margin_value = 0.2
pool_temp = 0.1

LN2 = math.log(2.0)
A = 1.0 / (pool_temp * LN2)
L = logit_scale * pool_temp
MARGIN2 = logit_scale * margin_value / LN2
INV_LN2 = 1.0 / LN2
OUT_SCALE = logit_scale * LN2

SUB = 3
E = 256
TC = 512
BB = 256
FT = 256
FC = 64
FB = 128
RC = 16
AWAY = -1e4
EXTRA = 16
GROUP = 8

DIM0 = (((0,), (0,)), ((), ()))
DIM1 = (((1,), (1,)), ((), ()))

f32 = jnp.float32
bf16 = jnp.bfloat16


def split3(x):
    hi = x.astype(bf16)
    rest = x - hi.astype(f32)
    mid = rest.astype(bf16)
    lo = (rest - mid.astype(f32)).astype(bf16)
    return hi, mid, lo


def inv_norm(floats):
    mean = jnp.sum(floats * floats, axis=-1, keepdims=True) * (1.0 / E)
    return lax.rsqrt(E * (mean + norm_eps))


def send_kernel(slot_ref, emb_ref, lab_ref, out_ref):
    rows = emb_ref[...].astype(f32)
    unit = (rows * inv_norm(rows)).astype(bf16)
    n = rows.shape[0]
    labels = lab_ref[...]
    lane = lax.broadcasted_iota(jnp.int32, (1, E), 1)
    wide = jnp.concatenate([labels] * (E // n), axis=1)
    mine = (lane >= slot_ref[0]) & (lane < slot_ref[0] + n)
    wide = jnp.where(mine, wide, 0)
    row = lax.broadcasted_iota(jnp.int32, (16, E), 0)
    digit = jnp.where(row == 0, wide & 127, jnp.where(row == 1, (wide >> 7) & 127, wide >> 14))
    digit = jnp.where(row < 3, digit, 0).astype(f32).astype(bf16)
    for j in range(out_ref.shape[0]):
        out_ref[j, pl.ds(0, n), :] = unit
        out_ref[j, pl.ds(n, 16), :] = digit


def centre_kernel(cent_ref, cb_ref):
    for k in range(SUB):
        rows = cent_ref[k].astype(f32)
        unit = rows * inv_norm(rows)
        cb_ref[0, pl.ds(k * TC, TC), :] = unit.astype(bf16)


def gather_kernel(rows_own, where_ref, got_ref, ut_ref, lab_ref, flag_ref):
    parts = got_ref.shape[0]
    per = E // rows_own
    for q in range(parts // per):
        digits = jnp.zeros((16, E), f32)
        for j in range(per):
            digits += got_ref[q * per + j, pl.ds(rows_own, 16), :].astype(f32)
        lab = digits[0:1] + 128.0 * digits[1:2] + 16384.0 * digits[2:3]
        lab_ref[:, pl.ds(q * E, E)] = lab.astype(jnp.int32)
        block = jnp.concatenate(
            [got_ref[q * per + j, pl.ds(0, rows_own), :].astype(f32) for j in range(per)], axis=0
        )
        ut_ref[:, pl.ds(q * E, E)] = block.T.astype(bf16)
    words, width = flag_ref.shape
    batch = lab_ref.shape[1]
    tile = (lab_ref[...] - where_ref[0]) >> (FC.bit_length() - 1)
    lane = lax.broadcasted_iota(jnp.int32, (words, width), 1)
    row = lax.broadcasted_iota(jnp.int32, (words, batch), 0) * (FT // FC)
    flags = jnp.zeros((words, width), jnp.int32)
    for i in range(FT // FC):
        hits = (row + i == tile).astype(f32)
        for b in range(batch // FB):
            some = jnp.sum(hits[:, b * FB : (b + 1) * FB], axis=1, keepdims=True) > 0
            j = b % (BB // FB)
            bit = jnp.where(some, 1 << (i * (BB // FB) + j), 0)
            flags += jnp.where(lane == b // (BB // FB), bit, 0)
    flag_ref[...] = flags


def elementwise(c0, c1, c2):
    d1 = (c1 - c0) * A
    d2 = (c2 - c0) * A
    e1 = jnp.exp2(d1)
    e2 = jnp.exp2(d2)
    r = 1.0 / (1.0 + e1 + e2)
    z = (e1 * d1 + e2 * d2) * r
    power = c0 * (L * A) + z * L
    shift = INV_LN2 - z
    return e1, e2, d1, d2, r, power, shift


def piece_of(i, h):
    per = BB // FB
    down = pl.multiple_of((i // per) * FC, FC) + h * FT
    return down, pl.multiple_of((i % per) * FB, FB)


def for_labels(flag_ref, step, batch, do):
    words = [
        (b, h, flag_ref[step * (TC // FT) + h, b])
        for b in range(batch // BB)
        for h in range(TC // FT)
    ]

    def look(b, h, word):
        def piece(i, carry):
            pl.when(((word >> i) & 1) > 0)(functools.partial(do, b, h, i))
            return carry

        lax.fori_loop(0, (FT // FC) * (BB // FB), piece, 0)

    @pl.when(functools.reduce(lambda x, y: x | y, [w for _, _, w in words]) > 0)
    def _():
        for b, h, word in words:
            pl.when(word > 0)(functools.partial(look, b, h, word))


def forward_kernel(
    first_ref, flag_ref, cb_ref, ut_ref, lab_ref,
    pt_ref, out_ref, target, own_ref, xs, sums, g1, g2, apart,
):
    step = pl.program_id(0)
    steps = pl.num_programs(0)
    batch = ut_ref.shape[1]

    @pl.when(step == 0)
    def _():
        sums[...] = jnp.zeros_like(sums)
        apart[...] = jnp.zeros_like(apart)
        g1[...] = jnp.zeros_like(g1)
        g2[...] = jnp.zeros_like(g2)

    first = first_ref[0] + step * TC
    tile_ref = pt_ref.at[step]

    def block(at, b):
        cols = pl.ds(b * BB, BB)
        xs[b] = jnp.dot(cb_ref[at], ut_ref[:, cols], preferred_element_type=f32)

    def set_labels_apart(b, h, i):
        down, over = piece_of(i, h)
        here = pl.ds(over, FB)
        cols = pl.ds(pl.multiple_of(over + b * BB, FB), FB)
        row = lax.broadcasted_iota(jnp.int32, (FC, FB), 0) + down
        hit = row == lab_ref[:, cols] - first
        found = [jnp.sum(jnp.where(hit, 1.0, 0.0), axis=0, keepdims=True)]
        for k in range(SUB):
            rows = pl.ds(pl.multiple_of(down + k * TC, FC), FC)
            v = xs[b, rows, here]
            found.append(jnp.sum(jnp.where(hit, v, 0.0), axis=0, keepdims=True))
            xs[b, rows, here] = jnp.where(hit, AWAY, v)
        apart[0:4, cols] += jnp.concatenate(found, axis=0)

    def label_rows(at, b, h, i):
        down, over = piece_of(i, h)
        cols = pl.ds(pl.multiple_of(over + b * BB, FB), FB)
        row = lax.broadcasted_iota(jnp.int32, (FC, FB), 0) + (down + at * TC + first_ref[0])
        hit = row == lab_ref[:, cols]
        own, rows = [], []
        for k in range(SUB):
            own.append(jnp.where(hit, own_ref[k : k + 1, cols], 0.0).astype(bf16))
            rows.append(cb_ref[at, pl.ds(pl.multiple_of(down + k * TC, FC), FC), :])
        own, rows = jnp.concatenate(own, axis=0), jnp.concatenate(rows, axis=0)
        g2[cols, :] += lax.dot_general(own, rows, DIM0, preferred_element_type=f32)

    def terms(b):
        cols = pl.ds(b * BB, BB)
        total = jnp.zeros((8, BB), f32)
        for c in range(TC // RC):
            x = [xs[b, pl.ds(k * TC + c * RC, RC), :] for k in range(SUB)]
            e1, e2, d1, d2, r, power, shift = elementwise(*x)
            ex = jnp.exp2(power)
            total += ex[0:8] + ex[8:16]
            g = ex * r
            p = (g * shift, (g * e1) * (d1 + shift), (g * e2) * (d2 + shift))
            for k in range(SUB):
                tile_ref[k, pl.ds(c * RC, RC), cols] = p[k].astype(bf16)
        sums[:, cols] += total

    def rows_sum(b):
        cols = pl.ds(b * BB, BB)
        p = jnp.concatenate([tile_ref[k, :, cols] for k in range(SUB)], axis=0)
        g1[:, cols] += lax.dot_general(cb_ref[step], p, DIM0, preferred_element_type=f32)

    @pl.when(step == 0)
    def _():
        for b in range(batch // BB):
            block(0, b)

    for_labels(flag_ref, step, batch, set_labels_apart)
    after = jnp.minimum(step + 1, steps - 1)
    for b in range(batch // BB):
        terms(b)
        block(after, b)
        rows_sum(b)

    @pl.when(step == steps - 1)
    def _():
        known = apart[0:1, :] > 0
        e1, e2, d1, d2, r, power, shift = elementwise(*(apart[k + 1 : k + 2, :] for k in range(SUB)))
        power = power - MARGIN2
        p = (r * shift, (r * e1) * (d1 + shift), (r * e2) * (d2 + shift))
        sums[0:1, :] += jnp.where(known, jnp.exp2(power), 0.0)
        none = jnp.zeros((8, batch), f32)
        target[...] = none
        own_ref[...] = none
        target[0:1, :] = jnp.where(known, power, 0.0)
        for k in range(SUB):
            own_ref[k : k + 1, :] = jnp.where(known, p[k], 0.0)

        def one(at, carry):
            for_labels(flag_ref, at, batch, functools.partial(label_rows, at))
            return carry

        lax.fori_loop(0, steps, one, 0)

    @pl.when(step == steps - 1)
    def _():
        parts = out_ref.shape[0]
        n = batch // parts
        per = E // n
        blocks = batch // E
        tot = jnp.sum(sums[...], axis=0, keepdims=True)
        tgt = jnp.sum(target[...], axis=0, keepdims=True)
        all_targets = jnp.sum(tgt, axis=1, keepdims=True)
        totals = jnp.concatenate([tot[:, q * E : (q + 1) * E] for q in range(blocks)], axis=0)
        for q in range(blocks):
            cols = slice(q * E, (q + 1) * E)
            a = g1[:, cols].T.astype(bf16)
            o = g2[q * E : (q + 1) * E, :].astype(bf16)
            extra = pack_extra(totals, tgt[:, cols], all_targets).astype(bf16)
            for j in range(per):
                out_ref[q * per + j, pl.ds(0, n), :] = a[j * n : (j + 1) * n]
                out_ref[q * per + j, pl.ds(n, n), :] = o[j * n : (j + 1) * n]
                out_ref[q * per + j, pl.ds(2 * n, EXTRA), :] = extra


def pack_extra(totals, target, all_targets):
    lane = lax.broadcasted_iota(jnp.int32, (1, E), 1)
    hi, mid, lo = split3(all_targets)
    tail = jnp.where(lane == 0, hi.astype(f32), jnp.where(lane == 1, mid.astype(f32), 0.0))
    tail = jnp.where(lane == 2, lo.astype(f32), tail)
    values = [v.astype(f32) for v in split3(totals)] + [v.astype(f32) for v in split3(target)]
    pad = EXTRA - 3 * totals.shape[0] - 4
    return jnp.concatenate(values + [tail] + [jnp.zeros((pad, E), f32)] * (pad > 0), axis=0)


def unpack_extra(extra, blocks):
    totals = extra[0:blocks] + extra[blocks : 2 * blocks] + extra[2 * blocks : 3 * blocks]
    m = 3 * blocks
    target = extra[m : m + 1] + extra[m + 1 : m + 2] + extra[m + 2 : m + 3]
    all_targets = jnp.sum(extra[m + 3 : m + 4], axis=1, keepdims=True)
    return totals, target, all_targets


def summed(got_ref):
    acc = got_ref[0].astype(f32)
    for j in range(1, got_ref.shape[0]):
        acc += got_ref[j].astype(f32)
    return acc


def middle_kernel(n, blocks, got_ref, out_ref):
    acc = summed(got_ref)
    extra = pack_extra(*unpack_extra(acc[2 * n :], blocks))
    others, height = out_ref.shape[0], out_ref.shape[1]
    m = n // GROUP
    pad = jnp.zeros((height - 2 * m - EXTRA, E), f32)
    for j in range(others):
        at = (j % GROUP) * m
        one = acc[at : at + m]
        two = acc[n + at : n + at + m]
        out_ref[j] = jnp.concatenate([one, two, extra] + [pad] * (pad.shape[0] > 0), axis=0).astype(bf16)


def rows_kernel(
    m, where_ref, got_ref, emb_ref, ut_ref, target_ref, own_ref,
    loss_ref, ust_ref, fac_ref, rows_ref,
):
    batch = ut_ref.shape[1]
    blocks = batch // E
    n = emb_ref.shape[0]
    acc = summed(got_ref)
    totals, target, all_targets = unpack_extra(acc[2 * m : 2 * m + EXTRA], blocks)
    tot = jnp.concatenate([totals[q : q + 1] for q in range(blocks)], axis=1)
    logs = jnp.sum(jnp.log(tot), axis=1, keepdims=True) - all_targets * LN2
    loss_ref[...] = logs * (1.0 / batch)
    inv = OUT_SCALE / tot
    ust_ref[...] = (ut_ref[...].astype(f32) * inv).astype(bf16)
    own_target = jnp.sum(target_ref[...], axis=0, keepdims=True)
    fac_ref[...] = own_ref[...] * (jnp.exp2(own_target) - tot)
    lane = lax.broadcasted_iota(jnp.int32, (m, batch), 1)
    row = lax.broadcasted_iota(jnp.int32, (m, batch), 0)
    inv_col = jnp.sum(jnp.where(lane == row + where_ref[1], inv, 0.0), axis=1, keepdims=True)
    lane = lax.broadcasted_iota(jnp.int32, (m, E), 1)
    row = lax.broadcasted_iota(jnp.int32, (m, E), 0)
    mine = lane == row + where_ref[2]
    t = jnp.sum(jnp.where(mine, target, 0.0), axis=1, keepdims=True)
    g = acc[0:m] * inv_col + acc[m : 2 * m] * (jnp.exp2(t) * inv_col - OUT_SCALE)
    lane = lax.broadcasted_iota(jnp.int32, (m, n), 1)
    row = lax.broadcasted_iota(jnp.int32, (m, n), 0)
    pick = jnp.where(lane == row + where_ref[3], 1.0, 0.0).astype(bf16)
    rows = jnp.dot(pick, emb_ref[...], preferred_element_type=f32)
    r = inv_norm(rows)
    unit = rows * r
    g = (g - unit * jnp.sum(unit * g, axis=1, keepdims=True)) * r
    for j in range(rows_ref.shape[0]):
        rows_ref[j] = g.astype(bf16)


def backward_kernel(
    first_ref, flag_ref, fac_ref, ust_ref, lab_ref, got_ref, cent_ref, pt_ref, ge_ref, gc_ref
):
    step = pl.program_id(0)
    batch = ust_ref.shape[1]
    first = first_ref[0] + step * TC

    @pl.when(step == 0)
    def _():
        parts = [got_ref[j].astype(f32) for j in range(got_ref.shape[0])]
        ge_ref[...] = jnp.concatenate(parts, axis=0).astype(bf16)

    def finish(rows, g):
        rows = rows.astype(f32)
        r = inv_norm(rows)
        unit = rows * r
        g = (g - unit * jnp.sum(unit * g, axis=1, keepdims=True)) * r
        return g.astype(bf16)

    def set_labels(b, h, i):
        down, over = piece_of(i, h)
        cols = pl.ds(pl.multiple_of(over + b * BB, FB), FB)
        row = lax.broadcasted_iota(jnp.int32, (FC, FB), 0) + down
        hit = row == lab_ref[:, cols] - first
        for k in range(SUB):
            v = pt_ref[step, k, pl.ds(down, FC), cols].astype(f32)
            v = jnp.where(hit, fac_ref[k : k + 1, cols], v)
            pt_ref[step, k, pl.ds(down, FC), cols] = v.astype(bf16)

    for_labels(flag_ref, step, batch, set_labels)
    for k in range(SUB):
        g = lax.dot_general(pt_ref[step, k], ust_ref[...], DIM1, preferred_element_type=f32)
        gc_ref[k] = finish(cent_ref[k], g)


def per_device(embeddings, labels, centres):
    n = embeddings.shape[0]
    parts = lax.axis_size("dp")
    others = lax.axis_size("cls")
    batch = n * parts
    blocks = batch // E
    local = centres.shape[1]
    steps = local // TC
    m = n // GROUP
    dp = lax.axis_index("dp")
    cls = lax.axis_index("cls")
    first = (dp * others + cls) * local
    slot = (dp & (E // n - 1)) * n
    at = (cls & (GROUP - 1)) * m
    where = jnp.stack([first, dp * n + at, slot + at, at]).astype(jnp.int32)
    smem = pl.BlockSpec(memory_space=pltpu.SMEM)
    vmem = pl.BlockSpec(memory_space=pltpu.VMEM)
    params = pltpu.CompilerParams(vmem_limit_bytes=30 * 1024 * 1024)
    shape = jax.ShapeDtypeStruct

    sent = pl.pallas_call(
        send_kernel,
        out_shape=shape((parts, n + 16, E), bf16),
        in_specs=[smem, vmem, vmem],
        out_specs=vmem,
    )(slot.astype(jnp.int32).reshape(1), embeddings, labels.reshape(1, n))
    got = lax.all_to_all(sent, "dp", 0, 0)
    tile = pl.BlockSpec((SUB, TC, E), lambda i: (0, i, 0))
    rows_tile = pl.BlockSpec((1, SUB * TC, E), lambda i: (i, 0, 0))
    cb = pl.pallas_call(
        centre_kernel,
        grid=(steps,),
        out_shape=shape((steps, SUB * TC, E), bf16),
        in_specs=[tile],
        out_specs=rows_tile,
        compiler_params=params,
        cost_estimate=pl.CostEstimate(flops=10**9, bytes_accessed=10**7, transcendentals=0),
    )(centres)
    ut, all_labels, flags = pl.pallas_call(
        functools.partial(gather_kernel, n),
        out_shape=(
            shape((E, batch), bf16),
            shape((1, batch), jnp.int32),
            shape((local // FT, 128), jnp.int32),
        ),
        in_specs=[smem, vmem],
        out_specs=(vmem, vmem, vmem),
        compiler_params=params,
    )(where, got)

    height = 2 * n + EXTRA
    pt, payload, own_target, own = pl.pallas_call(
        forward_kernel,
        grid=(steps,),
        out_shape=(
            shape((steps, SUB, TC, batch), bf16),
            shape((parts, height, E), bf16),
            shape((8, batch), f32),
            shape((8, batch), f32),
        ),
        in_specs=[smem, smem, vmem, vmem, vmem],
        out_specs=(vmem, vmem, vmem, vmem),
        scratch_shapes=[
            pltpu.VMEM((batch // BB, SUB * TC, BB), f32),
            pltpu.VMEM((8, batch), f32),
            pltpu.VMEM((E, batch), f32),
            pltpu.VMEM((batch, E), f32),
            pltpu.VMEM((8, batch), f32),
        ],
        compiler_params=params,
    )(where, flags, cb, ut, all_labels)

    got1 = lax.all_to_all(payload, "dp", 0, 0)
    second = pl.pallas_call(
        functools.partial(middle_kernel, n, blocks),
        out_shape=shape((others, 32, E), bf16),
        in_specs=[vmem],
        out_specs=vmem,
        compiler_params=params,
    )(got1)
    got2 = lax.all_to_all(second, "cls", 0, 0)
    loss, ust, fac, rows = pl.pallas_call(
        functools.partial(rows_kernel, m),
        out_shape=(
            shape((1, 1), f32),
            shape((E, batch), bf16),
            shape((8, batch), f32),
            shape((GROUP, m, E), bf16),
        ),
        in_specs=[smem, vmem, vmem, vmem, vmem, vmem],
        out_specs=(vmem, vmem, vmem, vmem),
        compiler_params=params,
    )(where, got2, embeddings, ut, own_target, own)
    groups = [list(range(g, g + GROUP)) for g in range(0, others, GROUP)]
    got3 = lax.all_to_all(rows, "cls", 0, 0, axis_index_groups=groups)
    grad_embeddings, grad_centres = pl.pallas_call(
        backward_kernel,
        grid=(steps,),
        out_shape=(shape((n, E), bf16), shape((SUB, local, E), bf16)),
        in_specs=[
            smem,
            smem,
            vmem,
            vmem,
            vmem,
            vmem,
            tile,
            vmem,
        ],
        out_specs=(vmem, tile),
        compiler_params=params,
    )(where, flags, fac, ust, all_labels, got3, centres, pt)
    return (loss.reshape(()), grad_embeddings, grad_centres)


def solution(mesh):
    return jax.shard_map(
        per_device,
        mesh=mesh,
        in_specs=(P("dp", None), P("dp"), P(None, ("dp", "cls"), None)),
        out_specs=(P(), P("dp", None), P(None, ("dp", "cls"), None)),
        check_vma=False,
    )
```

```python
import functools
import math

import jax
import jax.numpy as jnp
from jax import lax
from jax.experimental import pallas as pl
from jax.experimental.pallas import tpu as pltpu
from jax.sharding import PartitionSpec as P

norm_eps = 1e-06
logit_scale = 30.0
margin_value = 0.2
pool_temp = 0.1

LN2 = math.log(2.0)
A = 1.0 / (pool_temp * LN2)
L = logit_scale * pool_temp
MARGIN2 = logit_scale * margin_value / LN2
OUT_SCALE = logit_scale / pool_temp

SUB = 3
E = 256
TC = 512
BB = 256
FT = 256
FC = 64
FB = 128
RC = 16
AWAY = -1e4
EXTRA = 16
GROUP = 8

DIM0 = (((0,), (0,)), ((), ()))
DIM1 = (((1,), (1,)), ((), ()))

f32 = jnp.float32
bf16 = jnp.bfloat16


def split3(x):
    hi = x.astype(bf16)
    rest = x - hi.astype(f32)
    mid = rest.astype(bf16)
    lo = (rest - mid.astype(f32)).astype(bf16)
    return hi, mid, lo


def inv_norm(floats):
    mean = jnp.sum(floats * floats, axis=-1, keepdims=True) * (1.0 / E)
    return lax.rsqrt(E * (mean + norm_eps))


def send_kernel(slot_ref, emb_ref, lab_ref, out_ref):
    rows = emb_ref[...].astype(f32)
    unit = (rows * inv_norm(rows)).astype(bf16)
    n = rows.shape[0]
    labels = lab_ref[...]
    lane = lax.broadcasted_iota(jnp.int32, (1, E), 1)
    wide = jnp.concatenate([labels] * (E // n), axis=1)
    mine = (lane >= slot_ref[0]) & (lane < slot_ref[0] + n)
    wide = jnp.where(mine, wide, 0)
    row = lax.broadcasted_iota(jnp.int32, (16, E), 0)
    digit = jnp.where(row == 0, wide & 127, jnp.where(row == 1, (wide >> 7) & 127, wide >> 14))
    digit = jnp.where(row < 3, digit, 0).astype(f32).astype(bf16)
    for j in range(out_ref.shape[0]):
        out_ref[j, pl.ds(0, n), :] = unit
        out_ref[j, pl.ds(n, 16), :] = digit


def centre_kernel(cent_ref, cb_ref):
    for k in range(SUB):
        rows = cent_ref[k].astype(f32)
        unit = rows * inv_norm(rows)
        cb_ref[0, pl.ds(k * TC, TC), :] = unit.astype(bf16)


def gather_kernel(rows_own, where_ref, got_ref, ut_ref, lab_ref, flag_ref):
    parts = got_ref.shape[0]
    per = E // rows_own
    for q in range(parts // per):
        digits = jnp.zeros((16, E), f32)
        for j in range(per):
            digits += got_ref[q * per + j, pl.ds(rows_own, 16), :].astype(f32)
        lab = digits[0:1] + 128.0 * digits[1:2] + 16384.0 * digits[2:3]
        lab_ref[:, pl.ds(q * E, E)] = lab.astype(jnp.int32)
        block = jnp.concatenate(
            [got_ref[q * per + j, pl.ds(0, rows_own), :].astype(f32) for j in range(per)], axis=0
        )
        ut_ref[:, pl.ds(q * E, E)] = block.T.astype(bf16)
    words, width = flag_ref.shape
    batch = lab_ref.shape[1]
    tile = (lab_ref[...] - where_ref[0]) >> (FC.bit_length() - 1)
    lane = lax.broadcasted_iota(jnp.int32, (words, width), 1)
    row = lax.broadcasted_iota(jnp.int32, (words, batch), 0) * (FT // FC)
    flags = jnp.zeros((words, width), jnp.int32)
    for i in range(FT // FC):
        hits = (row + i == tile).astype(f32)
        for b in range(batch // FB):
            some = jnp.sum(hits[:, b * FB : (b + 1) * FB], axis=1, keepdims=True) > 0
            j = b % (BB // FB)
            bit = jnp.where(some, 1 << (i * (BB // FB) + j), 0)
            flags += jnp.where(lane == b // (BB // FB), bit, 0)
    flag_ref[...] = flags


def elementwise(c0, c1, c2):
    d1 = c1 - c0
    d2 = c2 - c0
    e1 = jnp.exp2(d1 * A)
    e2 = jnp.exp2(d2 * A)
    r = 1.0 / (1.0 + e1 + e2)
    z = (e1 * d1 + e2 * d2) * r
    power = (c0 + z) * (L * A)
    shift = pool_temp - z
    return e1, e2, d1, d2, r, power, shift


def piece_of(i, h):
    per = BB // FB
    return (i // per) * FC + h * FT, (i % per) * FB


def for_labels(flag_ref, step, batch, do):
    words = [
        (b, h, flag_ref[step * (TC // FT) + h, b])
        for b in range(batch // BB)
        for h in range(TC // FT)
    ]

    def look(b, h, word):
        for i in range((FT // FC) * (BB // FB)):
            pl.when((word & (1 << i)) > 0)(functools.partial(do, b, h, i))

    @pl.when(functools.reduce(lambda x, y: x | y, [w for _, _, w in words]) > 0)
    def _():
        for b, h, word in words:
            pl.when(word > 0)(functools.partial(look, b, h, word))


def forward_kernel(
    first_ref, flag_ref, cb_ref, ut_ref, lab_ref,
    pt_ref, out_ref, target, own_ref, xs, sums, g1, g2, apart,
):
    step = pl.program_id(0)
    steps = pl.num_programs(0)
    batch = ut_ref.shape[1]

    @pl.when(step == 0)
    def _():
        sums[...] = jnp.zeros_like(sums)
        apart[...] = jnp.zeros_like(apart)
        g1[...] = jnp.zeros_like(g1)
        g2[...] = jnp.zeros_like(g2)

    first = first_ref[0] + step * TC
    tile_ref = pt_ref.at[step]

    def block(at, b):
        cols = pl.ds(b * BB, BB)
        xs[b] = jnp.dot(cb_ref[at], ut_ref[:, cols], preferred_element_type=f32)

    def set_labels_apart(b, h, i):
        down, over = piece_of(i, h)
        here = pl.ds(over, FB)
        cols = pl.ds(over + b * BB, FB)
        row = lax.broadcasted_iota(jnp.int32, (FC, FB), 0) + down
        hit = row == lab_ref[:, cols] - first
        found = [jnp.sum(jnp.where(hit, 1.0, 0.0), axis=0, keepdims=True)]
        for k in range(SUB):
            rows = pl.ds(down + k * TC, FC)
            v = xs[b, rows, here]
            found.append(jnp.sum(jnp.where(hit, v, 0.0), axis=0, keepdims=True))
            xs[b, rows, here] = jnp.where(hit, AWAY, v)
        apart[0:4, cols] += jnp.concatenate(found, axis=0)

    def label_rows(at, b, h, i):
        down, over = piece_of(i, h)
        cols = pl.ds(over + b * BB, FB)
        row = lax.broadcasted_iota(jnp.int32, (FC, FB), 0) + (down + at * TC + first_ref[0])
        hit = row == lab_ref[:, cols]
        own, rows = [], []
        for k in range(SUB):
            own.append(jnp.where(hit, own_ref[k : k + 1, cols], 0.0).astype(bf16))
            rows.append(cb_ref[at, pl.ds(down + k * TC, FC), :])
        own, rows = jnp.concatenate(own, axis=0), jnp.concatenate(rows, axis=0)
        g2[cols, :] += lax.dot_general(own, rows, DIM0, preferred_element_type=f32)

    def terms(b):
        cols = pl.ds(b * BB, BB)
        total = jnp.zeros((8, BB), f32)
        for c in range(TC // RC):
            x = [xs[b, pl.ds(k * TC + c * RC, RC), :] for k in range(SUB)]
            e1, e2, d1, d2, r, power, shift = elementwise(*x)
            ex = jnp.exp2(power)
            total += ex[0:8] + ex[8:16]
            g = ex * r
            p = (g * shift, (g * e1) * (d1 + shift), (g * e2) * (d2 + shift))
            for k in range(SUB):
                tile_ref[k, pl.ds(c * RC, RC), cols] = p[k].astype(bf16)
        sums[:, cols] += total

    def rows_sum(b):
        cols = pl.ds(b * BB, BB)
        p = jnp.concatenate([tile_ref[k, :, cols] for k in range(SUB)], axis=0)
        g1[:, cols] += lax.dot_general(cb_ref[step], p, DIM0, preferred_element_type=f32)

    @pl.when(step == 0)
    def _():
        for b in range(batch // BB):
            block(0, b)

    for_labels(flag_ref, step, batch, set_labels_apart)
    after = jnp.minimum(step + 1, steps - 1)
    for b in range(batch // BB):
        terms(b)
        block(after, b)
        rows_sum(b)

    @pl.when(step == steps - 1)
    def _():
        known = apart[0:1, :] > 0
        e1, e2, d1, d2, r, power, shift = elementwise(*(apart[k + 1 : k + 2, :] for k in range(SUB)))
        power = power - MARGIN2
        p = (r * shift, (r * e1) * (d1 + shift), (r * e2) * (d2 + shift))
        sums[0:1, :] += jnp.where(known, jnp.exp2(power), 0.0)
        none = jnp.zeros((8, batch), f32)
        target[...] = none
        own_ref[...] = none
        target[0:1, :] = jnp.where(known, power, 0.0)
        for k in range(SUB):
            own_ref[k : k + 1, :] = jnp.where(known, p[k], 0.0)

        def one(at, carry):
            for_labels(flag_ref, at, batch, functools.partial(label_rows, at))
            return carry

        lax.fori_loop(0, steps, one, 0)

    @pl.when(step == steps - 1)
    def _():
        parts = out_ref.shape[0]
        n = batch // parts
        per = E // n
        blocks = batch // E
        tot = jnp.sum(sums[...], axis=0, keepdims=True)
        tgt = jnp.sum(target[...], axis=0, keepdims=True)
        all_targets = jnp.sum(tgt, axis=1, keepdims=True)
        totals = jnp.concatenate([tot[:, q * E : (q + 1) * E] for q in range(blocks)], axis=0)
        for q in range(blocks):
            cols = slice(q * E, (q + 1) * E)
            a = g1[:, cols].T.astype(bf16)
            o = g2[q * E : (q + 1) * E, :].astype(bf16)
            extra = pack_extra(totals, tgt[:, cols], all_targets).astype(bf16)
            for j in range(per):
                out_ref[q * per + j, pl.ds(0, n), :] = a[j * n : (j + 1) * n]
                out_ref[q * per + j, pl.ds(n, n), :] = o[j * n : (j + 1) * n]
                out_ref[q * per + j, pl.ds(2 * n, EXTRA), :] = extra


def pack_extra(totals, target, all_targets):
    lane = lax.broadcasted_iota(jnp.int32, (1, E), 1)
    hi, mid, lo = split3(all_targets)
    tail = jnp.where(lane == 0, hi.astype(f32), jnp.where(lane == 1, mid.astype(f32), 0.0))
    tail = jnp.where(lane == 2, lo.astype(f32), tail)
    values = [v.astype(f32) for v in split3(totals)] + [v.astype(f32) for v in split3(target)]
    pad = EXTRA - 3 * totals.shape[0] - 4
    return jnp.concatenate(values + [tail] + [jnp.zeros((pad, E), f32)] * (pad > 0), axis=0)


def unpack_extra(extra, blocks):
    totals = extra[0:blocks] + extra[blocks : 2 * blocks] + extra[2 * blocks : 3 * blocks]
    m = 3 * blocks
    target = extra[m : m + 1] + extra[m + 1 : m + 2] + extra[m + 2 : m + 3]
    all_targets = jnp.sum(extra[m + 3 : m + 4], axis=1, keepdims=True)
    return totals, target, all_targets


def summed(got_ref):
    acc = got_ref[0].astype(f32)
    for j in range(1, got_ref.shape[0]):
        acc += got_ref[j].astype(f32)
    return acc


def middle_kernel(n, blocks, got_ref, out_ref):
    acc = summed(got_ref)
    extra = pack_extra(*unpack_extra(acc[2 * n :], blocks))
    others, height = out_ref.shape[0], out_ref.shape[1]
    m = n // GROUP
    pad = jnp.zeros((height - 2 * m - EXTRA, E), f32)
    for j in range(others):
        at = (j % GROUP) * m
        one = acc[at : at + m]
        two = acc[n + at : n + at + m]
        out_ref[j] = jnp.concatenate([one, two, extra] + [pad] * (pad.shape[0] > 0), axis=0).astype(bf16)


def rows_kernel(
    m, where_ref, got_ref, emb_ref, ut_ref, target_ref, own_ref,
    loss_ref, ust_ref, fac_ref, rows_ref,
):
    batch = ut_ref.shape[1]
    blocks = batch // E
    n = emb_ref.shape[0]
    acc = summed(got_ref)
    totals, target, all_targets = unpack_extra(acc[2 * m : 2 * m + EXTRA], blocks)
    tot = jnp.concatenate([totals[q : q + 1] for q in range(blocks)], axis=1)
    logs = jnp.sum(jnp.log(tot), axis=1, keepdims=True) - all_targets * LN2
    loss_ref[...] = logs * (1.0 / batch)
    inv = OUT_SCALE / tot
    ust_ref[...] = (ut_ref[...].astype(f32) * inv).astype(bf16)
    own_target = jnp.sum(target_ref[...], axis=0, keepdims=True)
    fac_ref[...] = own_ref[...] * (jnp.exp2(own_target) - tot)
    lane = lax.broadcasted_iota(jnp.int32, (m, batch), 1)
    row = lax.broadcasted_iota(jnp.int32, (m, batch), 0)
    inv_col = jnp.sum(jnp.where(lane == row + where_ref[1], inv, 0.0), axis=1, keepdims=True)
    lane = lax.broadcasted_iota(jnp.int32, (m, E), 1)
    row = lax.broadcasted_iota(jnp.int32, (m, E), 0)
    mine = lane == row + where_ref[2]
    t = jnp.sum(jnp.where(mine, target, 0.0), axis=1, keepdims=True)
    g = acc[0:m] * inv_col + acc[m : 2 * m] * (jnp.exp2(t) * inv_col - OUT_SCALE)
    lane = lax.broadcasted_iota(jnp.int32, (m, n), 1)
    row = lax.broadcasted_iota(jnp.int32, (m, n), 0)
    pick = jnp.where(lane == row + where_ref[3], 1.0, 0.0).astype(bf16)
    rows = jnp.dot(pick, emb_ref[...], preferred_element_type=f32)
    r = inv_norm(rows)
    unit = rows * r
    g = (g - unit * jnp.sum(unit * g, axis=1, keepdims=True)) * r
    for j in range(rows_ref.shape[0]):
        rows_ref[j] = g.astype(bf16)


def backward_kernel(
    first_ref, flag_ref, fac_ref, ust_ref, lab_ref, got_ref, cent_ref, pt_ref, ge_ref, gc_ref
):
    step = pl.program_id(0)
    batch = ust_ref.shape[1]
    first = first_ref[0] + step * TC

    @pl.when(step == 0)
    def _():
        parts = [got_ref[j].astype(f32) for j in range(got_ref.shape[0])]
        ge_ref[...] = jnp.concatenate(parts, axis=0).astype(bf16)

    def finish(rows, g):
        rows = rows.astype(f32)
        r = inv_norm(rows)
        unit = rows * r
        g = (g - unit * jnp.sum(unit * g, axis=1, keepdims=True)) * r
        return g.astype(bf16)

    def set_labels(b, h, i):
        down, over = piece_of(i, h)
        cols = pl.ds(over + b * BB, FB)
        row = lax.broadcasted_iota(jnp.int32, (FC, FB), 0) + down
        hit = row == lab_ref[:, cols] - first
        for k in range(SUB):
            v = pt_ref[step, k, pl.ds(down, FC), cols].astype(f32)
            v = jnp.where(hit, fac_ref[k : k + 1, cols], v)
            pt_ref[step, k, pl.ds(down, FC), cols] = v.astype(bf16)

    for_labels(flag_ref, step, batch, set_labels)
    for k in range(SUB):
        g = lax.dot_general(pt_ref[step, k], ust_ref[...], DIM1, preferred_element_type=f32)
        gc_ref[k] = finish(cent_ref[k], g)


def per_device(embeddings, labels, centres):
    n = embeddings.shape[0]
    parts = lax.axis_size("dp")
    others = lax.axis_size("cls")
    batch = n * parts
    blocks = batch // E
    local = centres.shape[1]
    steps = local // TC
    m = n // GROUP
    dp = lax.axis_index("dp")
    cls = lax.axis_index("cls")
    first = (dp * others + cls) * local
    slot = (dp & (E // n - 1)) * n
    at = (cls & (GROUP - 1)) * m
    where = jnp.stack([first, dp * n + at, slot + at, at]).astype(jnp.int32)
    smem = pl.BlockSpec(memory_space=pltpu.SMEM)
    vmem = pl.BlockSpec(memory_space=pltpu.VMEM)
    params = pltpu.CompilerParams(vmem_limit_bytes=30 * 1024 * 1024)
    shape = jax.ShapeDtypeStruct

    sent = pl.pallas_call(
        send_kernel,
        out_shape=shape((parts, n + 16, E), bf16),
        in_specs=[smem, vmem, vmem],
        out_specs=vmem,
    )(slot.astype(jnp.int32).reshape(1), embeddings, labels.reshape(1, n))
    got = lax.all_to_all(sent, "dp", 0, 0)
    tile = pl.BlockSpec((SUB, TC, E), lambda i: (0, i, 0))
    rows_tile = pl.BlockSpec((1, SUB * TC, E), lambda i: (i, 0, 0))
    cb = pl.pallas_call(
        centre_kernel,
        grid=(steps,),
        out_shape=shape((steps, SUB * TC, E), bf16),
        in_specs=[tile],
        out_specs=rows_tile,
        compiler_params=params,
        cost_estimate=pl.CostEstimate(flops=10**9, bytes_accessed=10**7, transcendentals=0),
    )(centres)
    ut, all_labels, flags = pl.pallas_call(
        functools.partial(gather_kernel, n),
        out_shape=(
            shape((E, batch), bf16),
            shape((1, batch), jnp.int32),
            shape((local // FT, 128), jnp.int32),
        ),
        in_specs=[smem, vmem],
        out_specs=(vmem, vmem, vmem),
        compiler_params=params,
    )(where, got)

    height = 2 * n + EXTRA
    pt, payload, own_target, own = pl.pallas_call(
        forward_kernel,
        grid=(steps,),
        out_shape=(
            shape((steps, SUB, TC, batch), bf16),
            shape((parts, height, E), bf16),
            shape((8, batch), f32),
            shape((8, batch), f32),
        ),
        in_specs=[smem, smem, vmem, vmem, vmem],
        out_specs=(vmem, vmem, vmem, vmem),
        scratch_shapes=[
            pltpu.VMEM((batch // BB, SUB * TC, BB), f32),
            pltpu.VMEM((8, batch), f32),
            pltpu.VMEM((E, batch), f32),
            pltpu.VMEM((batch, E), f32),
            pltpu.VMEM((8, batch), f32),
        ],
        compiler_params=params,
    )(where, flags, cb, ut, all_labels)

    got1 = lax.all_to_all(payload, "dp", 0, 0)
    second = pl.pallas_call(
        functools.partial(middle_kernel, n, blocks),
        out_shape=shape((others, 32, E), bf16),
        in_specs=[vmem],
        out_specs=vmem,
        compiler_params=params,
    )(got1)
    got2 = lax.all_to_all(second, "cls", 0, 0)
    loss, ust, fac, rows = pl.pallas_call(
        functools.partial(rows_kernel, m),
        out_shape=(
            shape((1, 1), f32),
            shape((E, batch), bf16),
            shape((8, batch), f32),
            shape((GROUP, m, E), bf16),
        ),
        in_specs=[smem, vmem, vmem, vmem, vmem, vmem],
        out_specs=(vmem, vmem, vmem, vmem),
        compiler_params=params,
    )(where, got2, embeddings, ut, own_target, own)
    groups = [list(range(g, g + GROUP)) for g in range(0, others, GROUP)]
    got3 = lax.all_to_all(rows, "cls", 0, 0, axis_index_groups=groups)
    grad_embeddings, grad_centres = pl.pallas_call(
        backward_kernel,
        grid=(steps,),
        out_shape=(shape((n, E), bf16), shape((SUB, local, E), bf16)),
        in_specs=[
            smem,
            smem,
            vmem,
            vmem,
            vmem,
            vmem,
            tile,
            vmem,
        ],
        out_specs=(vmem, tile),
        compiler_params=params,
    )(where, flags, fac, ust, all_labels, got3, centres, pt)
    return (loss.reshape(()), grad_embeddings, grad_centres)


def solution(mesh):
    return jax.shard_map(
        per_device,
        mesh=mesh,
        in_specs=(P("dp", None), P("dp"), P(None, ("dp", "cls"), None)),
        out_specs=(P(), P("dp", None), P(None, ("dp", "cls"), None)),
        check_vma=False,
    )
```

```python
import functools
import math

import jax
import jax.numpy as jnp
from jax import lax
from jax.experimental import pallas as pl
from jax.experimental.pallas import tpu as pltpu
from jax.sharding import PartitionSpec as P

norm_eps = 1e-06
logit_scale = 30.0
margin_value = 0.2
pool_temp = 0.1

LN2 = math.log(2.0)
A = 1.0 / (pool_temp * LN2)
L = logit_scale * pool_temp
MARGIN2 = logit_scale * margin_value / LN2
OUT_SCALE = logit_scale / pool_temp

SUB = 3
E = 256
TC = 512
BB = 256
FT = 256
FC = 64
FB = 128
RC = 16
AWAY = -1e4
EXTRA = 16
GROUP = 8

DIM0 = (((0,), (0,)), ((), ()))
DIM1 = (((1,), (1,)), ((), ()))

f32 = jnp.float32
bf16 = jnp.bfloat16


def split3(x):
    hi = x.astype(bf16)
    rest = x - hi.astype(f32)
    mid = rest.astype(bf16)
    lo = (rest - mid.astype(f32)).astype(bf16)
    return hi, mid, lo


def inv_norm(floats):
    mean = jnp.sum(floats * floats, axis=-1, keepdims=True) * (1.0 / E)
    return lax.rsqrt(E * (mean + norm_eps))


def send_kernel(slot_ref, emb_ref, lab_ref, out_ref):
    rows = emb_ref[...].astype(f32)
    unit = rows * inv_norm(rows)
    n = rows.shape[0]
    labels = lab_ref[...]
    lane = lax.broadcasted_iota(jnp.int32, (1, E), 1)
    wide = jnp.concatenate([labels] * (E // n), axis=1)
    mine = (lane >= slot_ref[0]) & (lane < slot_ref[0] + n)
    wide = jnp.where(mine, wide, 0)
    row = lax.broadcasted_iota(jnp.int32, (8, E), 0)
    digit = jnp.where(row == 0, wide & 127, jnp.where(row == 1, (wide >> 7) & 127, wide >> 14))
    digit = jnp.where(row < 3, digit, 0).astype(f32)
    block = jnp.concatenate([unit, digit], axis=0).astype(bf16)
    for j in range(out_ref.shape[0]):
        out_ref[j] = block


def centre_kernel(cent_ref, cb_ref):
    for k in range(SUB):
        rows = cent_ref[k].astype(f32)
        unit = rows * inv_norm(rows)
        cb_ref[0, pl.ds(k * TC, TC), :] = unit.astype(bf16)


def gather_kernel(rows_own, where_ref, got_ref, ut_ref, lab_ref, flag_ref):
    parts = got_ref.shape[0]
    per = E // rows_own
    for q in range(parts // per):
        whole = [got_ref[q * per + j].astype(f32) for j in range(per)]
        digits = sum(w[rows_own:] for w in whole)
        lab = digits[0:1] + 128.0 * digits[1:2] + 16384.0 * digits[2:3]
        lab_ref[:, pl.ds(q * E, E)] = lab.astype(jnp.int32)
        block = jnp.concatenate([w[:rows_own] for w in whole], axis=0)
        ut_ref[:, pl.ds(q * E, E)] = block.T.astype(bf16)
    words, width = flag_ref.shape
    batch = lab_ref.shape[1]
    tile = (lab_ref[...] - where_ref[0]) >> (FC.bit_length() - 1)
    lane = lax.broadcasted_iota(jnp.int32, (words, width), 1)
    row = lax.broadcasted_iota(jnp.int32, (words, batch), 0) * (FT // FC)
    flags = jnp.zeros((words, width), jnp.int32)
    for i in range(FT // FC):
        hits = (row + i == tile).astype(f32)
        for b in range(batch // FB):
            some = jnp.sum(hits[:, b * FB : (b + 1) * FB], axis=1, keepdims=True) > 0
            j = b % (BB // FB)
            bit = jnp.where(some, 1 << (i * (BB // FB) + j), 0)
            flags += jnp.where(lane == b // (BB // FB), bit, 0)
    flag_ref[...] = flags


def elementwise(c0, c1, c2):
    d1 = c1 - c0
    d2 = c2 - c0
    e1 = jnp.exp2(d1 * A)
    e2 = jnp.exp2(d2 * A)
    r = 1.0 / (1.0 + e1 + e2)
    z = (e1 * d1 + e2 * d2) * r
    power = (c0 + z) * (L * A)
    shift = pool_temp - z
    return e1, e2, d1, d2, r, power, shift


def piece_of(i, h):
    per = BB // FB
    return (i // per) * FC + h * FT, (i % per) * FB


def for_labels(flag_ref, step, batch, do):
    words = [
        (b, h, flag_ref[step * (TC // FT) + h, b])
        for b in range(batch // BB)
        for h in range(TC // FT)
    ]

    def look(b, h, word):
        for i in range((FT // FC) * (BB // FB)):
            pl.when((word & (1 << i)) > 0)(functools.partial(do, b, h, i))

    @pl.when(functools.reduce(lambda x, y: x | y, [w for _, _, w in words]) > 0)
    def _():
        for b, h, word in words:
            pl.when(word > 0)(functools.partial(look, b, h, word))


def forward_kernel(
    first_ref, flag_ref, cb_ref, ut_ref, lab_ref,
    pt_ref, out_ref, target, own_ref, xs, sums, g1, g2, apart,
):
    step = pl.program_id(0)
    steps = pl.num_programs(0)
    batch = ut_ref.shape[1]

    @pl.when(step == 0)
    def _():
        sums[...] = jnp.zeros_like(sums)
        apart[...] = jnp.zeros_like(apart)
        g1[...] = jnp.zeros_like(g1)
        g2[...] = jnp.zeros_like(g2)

    first = first_ref[0] + step * TC
    tile_ref = pt_ref.at[step]

    def block(at, b):
        cols = pl.ds(b * BB, BB)
        xs[b] = jnp.dot(cb_ref[at], ut_ref[:, cols], preferred_element_type=f32)

    def set_labels_apart(b, h, i):
        down, over = piece_of(i, h)
        here = pl.ds(over, FB)
        cols = pl.ds(over + b * BB, FB)
        row = lax.broadcasted_iota(jnp.int32, (FC, FB), 0) + down
        hit = row == lab_ref[:, cols] - first
        found = [jnp.sum(jnp.where(hit, 1.0, 0.0), axis=0, keepdims=True)]
        for k in range(SUB):
            rows = pl.ds(down + k * TC, FC)
            v = xs[b, rows, here]
            found.append(jnp.sum(jnp.where(hit, v, 0.0), axis=0, keepdims=True))
            xs[b, rows, here] = jnp.where(hit, AWAY, v)
        apart[0:4, cols] += jnp.concatenate(found, axis=0)

    def label_rows(at, b, h, i):
        down, over = piece_of(i, h)
        cols = pl.ds(over + b * BB, FB)
        row = lax.broadcasted_iota(jnp.int32, (FC, FB), 0) + (down + at * TC + first_ref[0])
        hit = row == lab_ref[:, cols]
        own, rows = [], []
        for k in range(SUB):
            own.append(jnp.where(hit, own_ref[k : k + 1, cols], 0.0).astype(bf16))
            rows.append(cb_ref[at, pl.ds(down + k * TC, FC), :])
        own, rows = jnp.concatenate(own, axis=0), jnp.concatenate(rows, axis=0)
        g2[cols, :] += lax.dot_general(own, rows, DIM0, preferred_element_type=f32)

    def terms(b):
        cols = pl.ds(b * BB, BB)
        total = jnp.zeros((8, BB), f32)
        for c in range(TC // RC):
            x = [xs[b, pl.ds(k * TC + c * RC, RC), :] for k in range(SUB)]
            e1, e2, d1, d2, r, power, shift = elementwise(*x)
            ex = jnp.exp2(power)
            total += ex[0:8] + ex[8:16]
            g = ex * r
            p = (g * shift, (g * e1) * (d1 + shift), (g * e2) * (d2 + shift))
            for k in range(SUB):
                tile_ref[k, pl.ds(c * RC, RC), cols] = p[k].astype(bf16)
        sums[:, cols] += total

    def rows_sum(b):
        cols = pl.ds(b * BB, BB)
        p = jnp.concatenate([tile_ref[k, :, cols] for k in range(SUB)], axis=0)
        g1[:, cols] += lax.dot_general(cb_ref[step], p, DIM0, preferred_element_type=f32)

    @pl.when(step == 0)
    def _():
        for b in range(batch // BB):
            block(0, b)

    for_labels(flag_ref, step, batch, set_labels_apart)
    after = jnp.minimum(step + 1, steps - 1)
    for b in range(batch // BB):
        terms(b)
        block(after, b)
        rows_sum(b)

    @pl.when(step == steps - 1)
    def _():
        known = apart[0:1, :] > 0
        e1, e2, d1, d2, r, power, shift = elementwise(*(apart[k + 1 : k + 2, :] for k in range(SUB)))
        power = power - MARGIN2
        p = (r * shift, (r * e1) * (d1 + shift), (r * e2) * (d2 + shift))
        sums[0:1, :] += jnp.where(known, jnp.exp2(power), 0.0)
        none = jnp.zeros((8, batch), f32)
        target[...] = none
        own_ref[...] = none
        target[0:1, :] = jnp.where(known, power, 0.0)
        for k in range(SUB):
            own_ref[k : k + 1, :] = jnp.where(known, p[k], 0.0)

        def one(at, carry):
            for_labels(flag_ref, at, batch, functools.partial(label_rows, at))
            return carry

        lax.fori_loop(0, steps, one, 0)

    @pl.when(step == steps - 1)
    def _():
        parts = out_ref.shape[0]
        n = batch // parts
        per = E // n
        blocks = batch // E
        tot = jnp.sum(sums[...], axis=0, keepdims=True)
        tgt = jnp.sum(target[...], axis=0, keepdims=True)
        all_targets = jnp.sum(tgt, axis=1, keepdims=True)
        totals = jnp.concatenate([tot[:, q * E : (q + 1) * E] for q in range(blocks)], axis=0)
        for q in range(blocks):
            cols = slice(q * E, (q + 1) * E)
            a = g1[:, cols].T.astype(bf16)
            o = g2[q * E : (q + 1) * E, :].astype(bf16)
            extra = pack_extra(totals, tgt[:, cols], all_targets).astype(bf16)
            for j in range(per):
                out_ref[q * per + j, pl.ds(0, n), :] = a[j * n : (j + 1) * n]
                out_ref[q * per + j, pl.ds(n, n), :] = o[j * n : (j + 1) * n]
                out_ref[q * per + j, pl.ds(2 * n, EXTRA), :] = extra


def pack_extra(totals, target, all_targets):
    lane = lax.broadcasted_iota(jnp.int32, (1, E), 1)
    hi, mid, lo = split3(all_targets)
    tail = jnp.where(lane == 0, hi.astype(f32), jnp.where(lane == 1, mid.astype(f32), 0.0))
    tail = jnp.where(lane == 2, lo.astype(f32), tail)
    values = [v.astype(f32) for v in split3(totals)] + [v.astype(f32) for v in split3(target)]
    pad = EXTRA - 3 * totals.shape[0] - 4
    return jnp.concatenate(values + [tail] + [jnp.zeros((pad, E), f32)] * (pad > 0), axis=0)


def unpack_extra(extra, blocks):
    totals = extra[0:blocks] + extra[blocks : 2 * blocks] + extra[2 * blocks : 3 * blocks]
    m = 3 * blocks
    target = extra[m : m + 1] + extra[m + 1 : m + 2] + extra[m + 2 : m + 3]
    all_targets = jnp.sum(extra[m + 3 : m + 4], axis=1, keepdims=True)
    return totals, target, all_targets


def summed(got_ref):
    acc = got_ref[0].astype(f32)
    for j in range(1, got_ref.shape[0]):
        acc += got_ref[j].astype(f32)
    return acc


def middle_kernel(n, blocks, got_ref, out_ref):
    acc = summed(got_ref)
    extra = pack_extra(*unpack_extra(acc[2 * n :], blocks))
    others, height = out_ref.shape[0], out_ref.shape[1]
    m = n // GROUP
    pad = jnp.zeros((height - 2 * m - EXTRA, E), f32)
    for j in range(others):
        at = (j % GROUP) * m
        one = acc[at : at + m]
        two = acc[n + at : n + at + m]
        out_ref[j] = jnp.concatenate([one, two, extra] + [pad] * (pad.shape[0] > 0), axis=0).astype(bf16)


def rows_kernel(
    m, where_ref, got_ref, emb_ref, ut_ref, target_ref, own_ref,
    loss_ref, ust_ref, fac_ref, rows_ref,
):
    batch = ut_ref.shape[1]
    blocks = batch // E
    n = emb_ref.shape[0]
    acc = summed(got_ref)
    totals, target, all_targets = unpack_extra(acc[2 * m : 2 * m + EXTRA], blocks)
    tot = jnp.concatenate([totals[q : q + 1] for q in range(blocks)], axis=1)
    logs = jnp.sum(jnp.log(tot), axis=1, keepdims=True) - all_targets * LN2
    loss_ref[...] = logs * (1.0 / batch)
    inv = OUT_SCALE / tot
    ust_ref[...] = (ut_ref[...].astype(f32) * inv).astype(bf16)
    own_target = jnp.sum(target_ref[...], axis=0, keepdims=True)
    fac_ref[...] = own_ref[...] * (jnp.exp2(own_target) - tot)
    lane = lax.broadcasted_iota(jnp.int32, (m, batch), 1)
    row = lax.broadcasted_iota(jnp.int32, (m, batch), 0)
    inv_col = jnp.sum(jnp.where(lane == row + where_ref[1], inv, 0.0), axis=1, keepdims=True)
    lane = lax.broadcasted_iota(jnp.int32, (m, E), 1)
    row = lax.broadcasted_iota(jnp.int32, (m, E), 0)
    mine = lane == row + where_ref[2]
    t = jnp.sum(jnp.where(mine, target, 0.0), axis=1, keepdims=True)
    g = acc[0:m] * inv_col + acc[m : 2 * m] * (jnp.exp2(t) * inv_col - OUT_SCALE)
    lane = lax.broadcasted_iota(jnp.int32, (m, n), 1)
    row = lax.broadcasted_iota(jnp.int32, (m, n), 0)
    pick = jnp.where(lane == row + where_ref[3], 1.0, 0.0).astype(bf16)
    rows = jnp.dot(pick, emb_ref[...], preferred_element_type=f32)
    r = inv_norm(rows)
    unit = rows * r
    g = (g - unit * jnp.sum(unit * g, axis=1, keepdims=True)) * r
    for j in range(rows_ref.shape[0]):
        rows_ref[j] = g.astype(bf16)


def backward_kernel(
    first_ref, flag_ref, fac_ref, ust_ref, lab_ref, got_ref, cent_ref, pt_ref, ge_ref, gc_ref
):
    step = pl.program_id(0)
    batch = ust_ref.shape[1]
    first = first_ref[0] + step * TC

    @pl.when(step == 0)
    def _():
        parts = [got_ref[j].astype(f32) for j in range(got_ref.shape[0])]
        ge_ref[...] = jnp.concatenate(parts, axis=0).astype(bf16)

    def finish(rows, g):
        rows = rows.astype(f32)
        r = inv_norm(rows)
        unit = rows * r
        g = (g - unit * jnp.sum(unit * g, axis=1, keepdims=True)) * r
        return g.astype(bf16)

    def set_labels(b, h, i):
        down, over = piece_of(i, h)
        cols = pl.ds(over + b * BB, FB)
        row = lax.broadcasted_iota(jnp.int32, (FC, FB), 0) + down
        hit = row == lab_ref[:, cols] - first
        for k in range(SUB):
            v = pt_ref[step, k, pl.ds(down, FC), cols].astype(f32)
            v = jnp.where(hit, fac_ref[k : k + 1, cols], v)
            pt_ref[step, k, pl.ds(down, FC), cols] = v.astype(bf16)

    for_labels(flag_ref, step, batch, set_labels)
    for k in range(SUB):
        g = lax.dot_general(pt_ref[step, k], ust_ref[...], DIM1, preferred_element_type=f32)
        gc_ref[k] = finish(cent_ref[k], g)


def per_device(embeddings, labels, centres):
    n = embeddings.shape[0]
    parts = lax.axis_size("dp")
    others = lax.axis_size("cls")
    batch = n * parts
    blocks = batch // E
    local = centres.shape[1]
    steps = local // TC
    m = n // GROUP
    dp = lax.axis_index("dp")
    cls = lax.axis_index("cls")
    first = (dp * others + cls) * local
    slot = (dp & (E // n - 1)) * n
    at = (cls & (GROUP - 1)) * m
    where = jnp.stack([first, dp * n + at, slot + at, at]).astype(jnp.int32)
    smem = pl.BlockSpec(memory_space=pltpu.SMEM)
    vmem = pl.BlockSpec(memory_space=pltpu.VMEM)
    params = pltpu.CompilerParams(vmem_limit_bytes=30 * 1024 * 1024)
    shape = jax.ShapeDtypeStruct

    sent = pl.pallas_call(
        send_kernel,
        out_shape=shape((parts, n + 8, E), bf16),
        in_specs=[smem, vmem, vmem],
        out_specs=vmem,
    )(slot.astype(jnp.int32).reshape(1), embeddings, labels.reshape(1, n))
    got = lax.all_to_all(sent, "dp", 0, 0)
    tile = pl.BlockSpec((SUB, TC, E), lambda i: (0, i, 0))
    rows_tile = pl.BlockSpec((1, SUB * TC, E), lambda i: (i, 0, 0))
    cb = pl.pallas_call(
        centre_kernel,
        grid=(steps,),
        out_shape=shape((steps, SUB * TC, E), bf16),
        in_specs=[tile],
        out_specs=rows_tile,
        compiler_params=params,
        cost_estimate=pl.CostEstimate(flops=10**9, bytes_accessed=10**7, transcendentals=0),
    )(centres)
    ut, all_labels, flags = pl.pallas_call(
        functools.partial(gather_kernel, n),
        out_shape=(
            shape((E, batch), bf16),
            shape((1, batch), jnp.int32),
            shape((local // FT, 128), jnp.int32),
        ),
        in_specs=[smem, vmem],
        out_specs=(vmem, vmem, vmem),
        compiler_params=params,
    )(where, got)

    height = 2 * n + EXTRA
    pt, payload, own_target, own = pl.pallas_call(
        forward_kernel,
        grid=(steps,),
        out_shape=(
            shape((steps, SUB, TC, batch), bf16),
            shape((parts, height, E), bf16),
            shape((8, batch), f32),
            shape((8, batch), f32),
        ),
        in_specs=[smem, smem, vmem, vmem, vmem],
        out_specs=(vmem, vmem, vmem, vmem),
        scratch_shapes=[
            pltpu.VMEM((batch // BB, SUB * TC, BB), f32),
            pltpu.VMEM((8, batch), f32),
            pltpu.VMEM((E, batch), f32),
            pltpu.VMEM((batch, E), f32),
            pltpu.VMEM((8, batch), f32),
        ],
        compiler_params=params,
    )(where, flags, cb, ut, all_labels)

    got1 = lax.all_to_all(payload, "dp", 0, 0)
    second = pl.pallas_call(
        functools.partial(middle_kernel, n, blocks),
        out_shape=shape((others, 32, E), bf16),
        in_specs=[vmem],
        out_specs=vmem,
        compiler_params=params,
    )(got1)
    got2 = lax.all_to_all(second, "cls", 0, 0)
    loss, ust, fac, rows = pl.pallas_call(
        functools.partial(rows_kernel, m),
        out_shape=(
            shape((1, 1), f32),
            shape((E, batch), bf16),
            shape((8, batch), f32),
            shape((GROUP, m, E), bf16),
        ),
        in_specs=[smem, vmem, vmem, vmem, vmem, vmem],
        out_specs=(vmem, vmem, vmem, vmem),
        compiler_params=params,
    )(where, got2, embeddings, ut, own_target, own)
    groups = [list(range(g, g + GROUP)) for g in range(0, others, GROUP)]
    got3 = lax.all_to_all(rows, "cls", 0, 0, axis_index_groups=groups)
    grad_embeddings, grad_centres = pl.pallas_call(
        backward_kernel,
        grid=(steps,),
        out_shape=(shape((n, E), bf16), shape((SUB, local, E), bf16)),
        in_specs=[
            smem,
            smem,
            vmem,
            vmem,
            vmem,
            vmem,
            tile,
            vmem,
        ],
        out_specs=(vmem, tile),
        compiler_params=params,
    )(where, flags, fac, ust, all_labels, got3, centres, pt)
    return (loss.reshape(()), grad_embeddings, grad_centres)


def solution(mesh):
    return jax.shard_map(
        per_device,
        mesh=mesh,
        in_specs=(P("dp", None), P("dp"), P(None, ("dp", "cls"), None)),
        out_specs=(P(), P("dp", None), P(None, ("dp", "cls"), None)),
        check_vma=False,
    )
```
